32 devices in a mesh: tm: 16 (over z, x, core), tile: 2 (over y).
Axes of the slice: x: 2, y: 2, z: 4, core: 2. Of those that a mesh axis runs over, the one named last changes fastest.
Arguments:
- latent: bfloat16 [16, 4, 160, 384], P('tm', 'tile'), may hold values from -6 to 6
- gain: float32 [384], replicated, may hold values from 0.1 to 1.9
- conv_weight: bfloat16 [3, 3, 3, 384, 384], replicated, may hold values from -0.0625 to 0.0625
- conv_bias: float32 [384], replicated, may hold values from -3 to 3
- time_weight: bfloat16 [3, 384, 768], replicated, may hold values from -0.1875 to 0.1875
- time_bias: float32 [768], replicated, may hold values from -3 to 3
- up_weight: bfloat16 [3, 3, 384, 192], replicated, may hold values from -0.109375 to 0.109375
- up_bias: float32 [192], replicated, may hold values from -3 to 3
Outputs:
- decoded: bfloat16 [32, 8, 320, 192], P('tm', 'tile')
The draws below stay inside these ranges and needn't reach their ends.
All inputs are finite; a program needn't handle non-finite values.
Results may differ from the reference program's by a relative error of at most 0.0057.
Values may be sent and summed in bfloat16 or wider, within the bound.
No kernel may reach another device: no remote copies, remote signals or barrier semaphores. Data moves between devices by JAX's collectives and lax.ppermute only.
A program may use at most 64 MiB of HBM per device.

```python
import jax
import jax.numpy as jnp
from jax import lax

C = 384
CO = 192
COLS = 160
FRAMES = 16
ROWS = 4


def block_scale(key, extent, shards, least, top_value):
    level = 1.0
    for position, parts in shards:
        draws = jax.random.uniform(jax.random.fold_in(jax.random.fold_in(key, 6), position), (parts,), jnp.float32, least / len(shards), top_value / len(shards))
        level = level * jnp.repeat(jnp.exp(draws), extent[position] // parts).reshape((-1,) + (1,) * (len(extent) - 1 - position))
    return level


def gaussian(own_key, shape, scale, bound, pieces=(), held_as=jnp.bfloat16):
    drawn = jax.random.normal(own_key, shape, jnp.float32) * scale
    if len(pieces) > 0:
        drawn = block_scale(own_key, shape, pieces, -0.22, 0.18) * drawn
    return jnp.clip(drawn, min=-bound, max=bound).astype(held_as)


def setup_inputs(seed: int = 0) -> dict:
    arg_keys = jax.random.split(jax.random.key(seed), 9)
    latent = gaussian(arg_keys[0], (FRAMES, ROWS, COLS, C), 1.0, 6.0, ((0, 16), (1, 2)))
    gain = jnp.clip(1.0 + 0.18 * jax.random.normal(arg_keys[1], (C,), jnp.float32), 0.1, 1.9)
    conv_weight = gaussian(arg_keys[2], (3, 3, 3, C, C), (27 * C) ** -0.5, 0.0625)
    conv_bias = gaussian(arg_keys[3], (C,), 0.5, 3.0, (), jnp.float32)
    time_weight = gaussian(arg_keys[4], (3, C, 2 * C), (3 * C) ** -0.5, 0.1875)
    time_bias = gaussian(arg_keys[5], (2 * C,), 0.5, 3.0, (), jnp.float32)
    up_weight = gaussian(arg_keys[6], (3, 3, C, CO), (9 * C) ** -0.5, 0.109375)
    up_bias = gaussian(arg_keys[7], (CO,), 0.5, 3.0, (), jnp.float32)
    return dict(latent=latent, gain=gain, conv_weight=conv_weight, conv_bias=conv_bias, time_weight=time_weight, time_bias=time_bias, up_weight=up_weight, up_bias=up_bias)


def activate(field, gain):
    values = field.astype(jnp.float32)
    meansq = lax.optimization_barrier(jnp.mean(values * values, axis=-1, keepdims=True))
    scaled = values * lax.rsqrt(meansq + 1e-06) * gain
    return (scaled * jax.nn.sigmoid(scaled)).astype(jnp.bfloat16)

def reference(latent, gain, conv_weight, conv_bias, time_weight, time_bias, up_weight, up_bias):
    activated = activate(latent, gain)
    summed = lax.conv_general_dilated(activated.astype(jnp.float32)[None], conv_weight.astype(jnp.float32), (1, 1, 1), ((2, 0), (1, 1), (1, 1)), dimension_numbers=('NDHWC', 'DHWIO', 'NDHWC'), precision=lax.Precision.HIGHEST)[0]
    block = (summed + conv_bias + latent.astype(jnp.float32)).astype(jnp.bfloat16)
    mixed = lax.conv_general_dilated(block.astype(jnp.float32)[None], time_weight.astype(jnp.float32)[:, None, None], (1, 1, 1), ((2, 0), (0, 0), (0, 0)), dimension_numbers=('NDHWC', 'DHWIO', 'NDHWC'), precision=lax.Precision.HIGHEST)[0]
    doubled = (mixed + time_bias).astype(jnp.bfloat16)
    frames_n, rows_n, cols_n, chans = block.shape
    frames = doubled.reshape(frames_n, rows_n, cols_n, 2, chans).transpose(0, 3, 1, 2, 4).reshape(2 * frames_n, rows_n, cols_n, chans)
    kernel = up_weight.astype(jnp.float32)

    def one_frame(frame):
        upsampled = jnp.repeat(jnp.repeat(frame, 2, axis=0), 2, axis=1).astype(jnp.float32)
        result = lax.conv_general_dilated(upsampled[None], kernel, (1, 1), ((1, 1), (1, 1)), dimension_numbers=('NHWC', 'HWIO', 'NHWC'), precision=lax.Precision.HIGHEST)[0]
        return (result + up_bias).astype(jnp.bfloat16)
    return lax.map(one_frame, frames)
```

```python
import functools

import jax
import jax.numpy as jnp
from jax import lax
from jax.experimental import pallas as pl
from jax.experimental.pallas import tpu as pltpu
from jax.sharding import PartitionSpec as P

F32 = jnp.float32
BF16 = jnp.bfloat16
VMEM = pl.BlockSpec(memory_space=pltpu.VMEM)
SMEM = pl.BlockSpec(memory_space=pltpu.SMEM)
ANY = pl.BlockSpec(memory_space=pl.ANY)


def activate(rows, gain):
    values = rows.astype(F32)
    meansq = jnp.mean(values * values, axis=-1, keepdims=True)
    scaled = values * lax.rsqrt(meansq + 1e-06) * gain
    return (scaled * jax.nn.sigmoid(scaled)).astype(BF16)


def moved(rows, step):
    cols = rows.shape[0]
    index = lax.broadcasted_iota(jnp.int32, rows.shape, 0)
    edge = 0 if step == 1 else cols - 1
    return jnp.where(index == edge, 0.0, pltpu.roll(rows, step % cols, 0))


def conv_kernel(halos, place, own, edges, main2, edges2, packed1, gain, bias, w_hbm, block, near, wbuf, act, sems):
    flip = place[0]
    rows, cols, chans = own.shape
    lead = halos - 1

    def copies(dt):
        return [
            pltpu.make_async_copy(
                w_hbm.at[dt, jnp.where(flip == 1, 2 - dh, dh), dw],
                wbuf.at[dt, pl.ds(dh * chans, chans), pl.ds(dw * chans, chans)],
                sems.at[dt, dh, dw],
            )
            for dh in range(3)
            for dw in range(3)
        ]

    order = (2, 0, 1)
    for dt in order:
        for copy in copies(dt):
            copy.start()

    scale = gain[...]
    mains = {2: own, 0: main2, 1: packed1}
    for dt in order:
        for q in range(rows):
            act[dt, lead + q] = activate(mains[dt][jnp.where(flip == 1, rows - 1 - q, q)], scale)
        for h in range(halos):
            source = {2: edges, 0: edges2}[dt][h] if dt != 1 else packed1[rows + h]
            act[dt, 0 if h < lead else lead + rows] = activate(source, scale)

    totals = [None] * rows
    for dt in order:
        for copy in copies(dt):
            copy.wait()
        for q in range(rows):
            first = max(lead + q - 1, 0)
            last = lead + q + 1
            left = jnp.concatenate([act[dt, s] for s in range(first, last + 1)], axis=-1)
            dh0 = first - (lead + q - 1)
            part = jnp.dot(left, wbuf[dt, dh0 * chans :, :], preferred_element_type=F32)
            totals[q] = part if totals[q] is None else totals[q] + part

    for q in range(rows):
        total = totals[q]
        mixed = (
            total[:, chans : 2 * chans]
            + moved(total[:, :chans], 1)
            + moved(total[:, 2 * chans :], -1)
        )
        where = jnp.where(flip == 1, rows - 1 - q, q)
        value = (mixed + bias[...] + own[where].astype(F32)).astype(BF16)
        block[where] = value
        if halos == 1:
            if q == rows - 1:
                near[0] = value
        else:
            if q == 0:
                near[0] = value
            if q == rows - 1:
                near[1] = value


def up_kernel(halos, place, own, edges, main2, edges2, packed1, tbias, ubias, tw_hbm, uw_hbm, out_hbm,
              tw, uw, doubled, wide, outs, sems, osems):
    flip = place[0]
    rows, cols, chans = own.shape
    lead = halos - 1
    count = rows + halos
    outs_n = ubias.shape[-1]
    lanes = 128
    rest = outs_n - lanes
    load_t = pltpu.make_async_copy(tw_hbm, tw, sems.at[0])
    load_u = pltpu.make_async_copy(uw_hbm, uw, sems.at[1])
    load_t.start()
    load_u.start()

    def row_of(dt, s):
        if lead <= s < lead + rows:
            q = s - lead
            main = {2: own, 0: main2, 1: packed1}[dt]
            return main[jnp.where(flip == 1, rows - 1 - q, q)]
        h = 0 if s < lead else halos - 1
        return packed1[rows + h] if dt == 1 else {2: edges, 0: edges2}[dt][h]

    left = jnp.concatenate(
        [jnp.concatenate([row_of(dt, s) for dt in range(3)], axis=-1) for s in range(count)], axis=0
    )
    load_t.wait()
    mixed = jnp.dot(left, tw[...], preferred_element_type=F32) + tbias[...]
    for s in range(count):
        value = mixed[s * cols : (s + 1) * cols]
        if halos == 2 and s == 0:
            value = jnp.where(place[1] == 1, value, 0.0)
        if halos == 2 and s == count - 1:
            value = jnp.where(place[2] == 1, value, 0.0)
        for f in range(2):
            doubled[f, s] = value[:, f * chans : (f + 1) * chans].astype(BF16)

    load_u.wait()
    lane = lax.broadcasted_iota(jnp.int32, (cols, lanes), 1)
    stores = []
    for q in range(rows):
        for phase in range(2):
            s = lead + q
            taken = [r for r in (s - 1 + phase, s + phase) if r >= 0]
            left = jnp.concatenate(
                [jnp.concatenate([doubled[f, r] for r in taken], axis=-1) for f in range(2)], axis=0
            )
            right = uw[phase, (2 - len(taken)) * chans :, :]
            both = jnp.dot(left, right, preferred_element_type=F32)
            for f in range(2):
                part = both[f * cols : (f + 1) * cols]
                g = [part[:, k * lanes : (k + 1) * lanes] for k in range(6)]
                even = g[0] + moved(g[2], 1) + ubias[:, :lanes]
                odd = g[1] + moved(g[3], -1) + ubias[:, :lanes]
                tail = g[4] + jnp.where(lane < rest, moved(g[5], 1), moved(g[5], -1))
                wide[0, pl.ds(0, cols, stride=2), :] = even
                wide[0, pl.ds(1, cols, stride=2), :] = odd
                wide[1, pl.ds(0, cols, stride=2), :] = tail
                wide[1, pl.ds(1, cols, stride=2), :] = pltpu.roll(tail, lanes - rest, 1)
                o = 2 * q + phase
                outs[f, o, :, :lanes] = wide[0].astype(BF16)
                outs[f, o, :, lanes:] = (wide[1, :, :rest] + ubias[:, lanes:]).astype(BF16)
                copy = pltpu.make_async_copy(
                    outs.at[f, o],
                    out_hbm.at[f, jnp.where(flip == 1, 2 * rows - 1 - o, o)],
                    osems.at[f, o],
                )
                copy.start()
                stores.append(copy)
    for copy in stores:
        copy.wait()


def merged_taps(up_weight, flip):
    taps = up_weight.astype(F32)
    taps = jnp.where(flip == 1, taps[::-1], taps)
    near = jnp.stack([jnp.stack([taps[0], taps[1] + taps[2]]), jnp.stack([taps[0] + taps[1], taps[2]])])
    e0, e12 = near[:, :, 0], near[:, :, 1] + near[:, :, 2]
    o01, o2 = near[:, :, 0] + near[:, :, 1], near[:, :, 2]
    lanes = 128
    wide = jnp.concatenate(
        [a[..., :lanes] for a in (e12, o01, e0, o2)] + [a[..., lanes:] for a in (e12, o01, e0, o2)], axis=-1
    )
    return wide.astype(BF16).reshape(2, -1, wide.shape[-1])


def exchange(main, near, halos, core):
    frames = lax.axis_size("tm")
    tiles = lax.axis_size("tile")
    later = [(i, i + 2) for i in range(frames - 2)]
    main2 = lax.ppermute(main, "tm", later)
    if halos == 1:
        sides = [(near[0], [(0, 1), (1, 0)])]
    else:
        sides = [
            (near[1], [(j, j + 1) for j in range(tiles - 1)]),
            (near[0], [(j + 1, j) for j in range(tiles - 1)]),
        ]
    edges = jnp.stack([lax.ppermute(row, "tile", route) for row, route in sides])
    edges2 = jnp.stack(
        [
            lax.ppermute(
                row,
                ("tm", "tile"),
                [(a * tiles + i, b * tiles + j) for a, b in later for i, j in route],
            )
            for row, route in sides
        ]
    )
    packed = jnp.where(core == 0, jnp.concatenate([main, edges]), jnp.concatenate([main2, edges2]))
    packed1 = lax.ppermute(packed, "tm", [(i, i ^ 1) for i in range(frames)])
    return main, edges, main2, edges2, packed1


def local(latent, gain, conv_weight, conv_bias, time_weight, time_bias, up_weight, up_bias):
    tiles = lax.axis_size("tile")
    tile = lax.axis_index("tile")
    core = lax.axis_index("tm") % 2
    halos = 1 if tiles == 2 else 2
    main = latent[0]
    rows, cols, chans = main.shape
    outs_n = up_weight.shape[3]
    flip = tile if halos == 1 else 0 * tile
    place = jnp.stack([flip, tile > 0, tile < tiles - 1]).astype(jnp.int32)
    up_w = merged_taps(up_weight, flip)

    if halos == 1:
        near = [lax.dynamic_index_in_dim(main, (rows - 1) * (1 - tile), 0, keepdims=False)]
    else:
        near = [main[0], main[rows - 1]]

    args = exchange(main, near, halos, core)
    block, near = pl.pallas_call(
        functools.partial(conv_kernel, halos),
        out_shape=(
            jax.ShapeDtypeStruct((rows, cols, chans), BF16),
            jax.ShapeDtypeStruct((halos, cols, chans), BF16),
        ),
        in_specs=[SMEM] + [VMEM] * 7 + [ANY],
        out_specs=(VMEM, VMEM),
        scratch_shapes=[
            pltpu.VMEM((3, 3 * chans, 3 * chans), BF16),
            pltpu.VMEM((3, rows + halos, cols, chans), BF16),
            pltpu.SemaphoreType.DMA((3, 3, 3)),
        ],
        compiler_params=pltpu.CompilerParams(vmem_limit_bytes=48 << 20),
        cost_estimate=pl.CostEstimate(flops=2500000000, bytes_accessed=9000000, transcendentals=600000),
    )(place, *args, gain[None], conv_bias[None], conv_weight)

    args = exchange(block, [near[h] for h in range(halos)], halos, core)
    return pl.pallas_call(
        functools.partial(up_kernel, halos),
        out_shape=jax.ShapeDtypeStruct((2, 2 * rows, 2 * cols, outs_n), BF16),
        in_specs=[SMEM] + [VMEM] * 7 + [ANY] * 2,
        out_specs=ANY,
        scratch_shapes=[
            pltpu.VMEM((3 * chans, 2 * chans), BF16),
            pltpu.VMEM((2, 2 * chans, 4 * outs_n), BF16),
            pltpu.VMEM((2, rows + halos, cols, chans), BF16),
            pltpu.VMEM((2, 2 * cols, 128), F32),
            pltpu.VMEM((2, 2 * rows, 2 * cols, outs_n), BF16),
            pltpu.SemaphoreType.DMA((2,)),
            pltpu.SemaphoreType.DMA((2, 2 * rows)),
        ],
        compiler_params=pltpu.CompilerParams(vmem_limit_bytes=48 << 20),
        cost_estimate=pl.CostEstimate(flops=2500000000, bytes_accessed=6000000, transcendentals=0),
    )(place, *args, time_bias[None], up_bias[None], time_weight.reshape(3 * chans, 2 * chans), up_w)


def solution(mesh):
    placed = (P("tm", "tile", None, None), P(), P(), P(), P(), P(), P(), P())
    return jax.shard_map(
        local, mesh=mesh, in_specs=placed, out_specs=P("tm", "tile", None, None), check_vma=False
    )
```

```python
import functools

import jax
import jax.numpy as jnp
from jax import lax
from jax.experimental import pallas as pl
from jax.experimental.pallas import tpu as pltpu
from jax.sharding import PartitionSpec as P

F32 = jnp.float32
BF16 = jnp.bfloat16
VMEM = pl.BlockSpec(memory_space=pltpu.VMEM)
SMEM = pl.BlockSpec(memory_space=pltpu.SMEM)
ANY = pl.BlockSpec(memory_space=pl.ANY)


def activate(rows, gain):
    values = rows.astype(F32)
    meansq = jnp.mean(values * values, axis=-1, keepdims=True)
    scaled = values * lax.rsqrt(meansq + 1e-06) * gain
    return (scaled * jax.nn.sigmoid(scaled)).astype(BF16)


def moved(rows, step):
    cols = rows.shape[0]
    index = lax.broadcasted_iota(jnp.int32, rows.shape, 0)
    edge = 0 if step == 1 else cols - 1
    return jnp.where(index == edge, 0.0, pltpu.roll(rows, step % cols, 0))


def conv_part(halos, flip, dt, main, edges, gain, weight, act):
    rows, cols, chans = main.shape
    lead = halos - 1
    for q in range(rows):
        act[lead + q] = activate(main[jnp.where(flip == 1, rows - 1 - q, q)], gain)
    for h in range(halos):
        act[0 if h < lead else lead + rows] = activate(edges[h], gain)
    parts = []
    for q in range(rows):
        first = max(lead + q - 1, 0)
        taken = range(first, lead + q + 2)
        left = jnp.concatenate([act[s] for s in taken], axis=-1)
        taps = [s - (lead + q - 1) for s in taken]
        right = jnp.concatenate(
            [
                jnp.concatenate([weight[dt, jnp.where(flip == 1, 2 - dh, dh), dw] for dw in range(3)], axis=-1)
                for dh in taps
            ],
            axis=0,
        )
        total = jnp.dot(left, right, preferred_element_type=F32)
        parts.append(
            total[:, chans : 2 * chans]
            + moved(total[:, :chans], 1)
            + moved(total[:, 2 * chans :], -1)
        )
    return parts


def conv_first(halos, place, own, edges, gain, bias, weight, acc, act):
    flip = place[0]
    rows = own.shape[0]
    for q, part in enumerate(conv_part(halos, flip, 2, own, edges, gain[...], weight, act)):
        acc[q] = part + bias[...] + own[jnp.where(flip == 1, rows - 1 - q, q)].astype(F32)


def conv_second(halos, place, main, edges, before, gain, weight, acc, act):
    for q, part in enumerate(conv_part(halos, place[0], 0, main, edges, gain[...], weight, act)):
        acc[q] = before[q] + part


def conv_third(halos, place, main_a, edges_a, main_b, edges_b, before, gain, weight, block, near, act, main, edges):
    flip = place[0]
    rows = block.shape[0]
    pick(place, main_a, edges_a, main_b, edges_b, main, edges)
    for q, part in enumerate(conv_part(halos, flip, 1, main, edges, gain[...], weight, act)):
        value = (before[q] + part).astype(BF16)
        block[jnp.where(flip == 1, rows - 1 - q, q)] = value
        if q == rows - 1:
            near[halos - 1] = value
        if q == 0 and halos == 2:
            near[0] = value


def pick(place, main_a, edges_a, main_b, edges_b, main, edges):
    @pl.when(place[3] == 0)
    def _():
        main[...] = main_a[...]
        edges[...] = edges_a[...]

    @pl.when(place[3] != 0)
    def _():
        main[...] = main_b[...]
        edges[...] = edges_b[...]


def up_kernel(halos, place, own, edges, main2, edges2, main_a, edges_a, main_b, edges_b, tbias, ubias, tw, uw,
              out_hbm, main1, edges1, doubled, wide, outs, osems):
    flip = place[0]
    rows, cols, chans = own.shape
    lead = halos - 1
    count = rows + halos
    lanes = 128
    rest = ubias.shape[-1] - lanes
    pick(place, main_a, edges_a, main_b, edges_b, main1, edges1)
    mains = (main2, main1, own)
    sides = (edges2, edges1, edges)

    def row_of(dt, s):
        if lead <= s < lead + rows:
            q = s - lead
            return mains[dt][jnp.where(flip == 1, rows - 1 - q, q)]
        return sides[dt][0 if s < lead else halos - 1]

    left = jnp.concatenate(
        [jnp.concatenate([row_of(dt, s) for dt in range(3)], axis=-1) for s in range(count)], axis=0
    )
    mixed = jnp.dot(left, tw[...], preferred_element_type=F32) + tbias[...]
    for s in range(count):
        value = mixed[s * cols : (s + 1) * cols]
        if halos == 2 and s == 0:
            value = jnp.where(place[1] == 1, value, 0.0)
        if halos == 2 and s == count - 1:
            value = jnp.where(place[2] == 1, value, 0.0)
        for f in range(2):
            doubled[f, s] = value[:, f * chans : (f + 1) * chans].astype(BF16)

    lane = lax.broadcasted_iota(jnp.int32, (cols, lanes), 1)
    stores = []
    for q in range(rows):
        for phase in range(2):
            s = lead + q
            taken = [r for r in (s - 1 + phase, s + phase) if r >= 0]
            left = jnp.concatenate(
                [jnp.concatenate([doubled[f, r] for r in taken], axis=-1) for f in range(2)], axis=0
            )
            right = uw[phase, (2 - len(taken)) * chans :, :]
            both = jnp.dot(left, right, preferred_element_type=F32)
            for f in range(2):
                part = both[f * cols : (f + 1) * cols]
                g = [part[:, k * lanes : (k + 1) * lanes] for k in range(6)]
                tail = g[4] + jnp.where(lane < rest, moved(g[5], 1), moved(g[5], -1))
                o = 2 * q + phase
                slot = (2 * o + f) % 2
                wide[slot, 0, pl.ds(0, cols, stride=2), :] = g[0] + moved(g[2], 1) + ubias[:, :lanes]
                wide[slot, 0, pl.ds(1, cols, stride=2), :] = g[1] + moved(g[3], -1) + ubias[:, :lanes]
                wide[slot, 1, pl.ds(0, cols, stride=2), :] = tail
                wide[slot, 1, pl.ds(1, cols, stride=2), :] = pltpu.roll(tail, lanes - rest, 1)
                outs[f, o, :lanes, :] = wide[slot, 0].T.astype(BF16)
                outs[f, o, lanes:, :] = (wide[slot, 1, :, :rest] + ubias[:, lanes:]).T.astype(BF16)
                copy = pltpu.make_async_copy(
                    outs.at[f, o],
                    out_hbm.at[f, jnp.where(flip == 1, 2 * rows - 1 - o, o)],
                    osems.at[f, o],
                )
                copy.start()
                stores.append(copy)
    for copy in stores:
        copy.wait()


def merge_kernel(place, taps, merged):
    flip = place[0]
    lanes = 128
    chans = taps.shape[3]

    def tap(dh, dw):
        return taps[jnp.where(flip == 1, 2 - dh, dh), dw].astype(F32)

    for phase, sets in enumerate((((0,), (1, 2)), ((0, 1), (2,)))):
        for which, rows in enumerate(sets):
            cols = [sum(tap(dh, dw) for dh in rows) for dw in range(3)]
            groups = (cols[1] + cols[2], cols[0] + cols[1], cols[0], cols[2])
            wide = jnp.concatenate([g[:lanes] for g in groups] + [g[lanes:] for g in groups], axis=0)
            merged[phase, which * chans : (which + 1) * chans, :] = wide.T.astype(BF16)


def exchange(main, near, halos):
    frames = lax.axis_size("tm")
    tiles = lax.axis_size("tile")
    later = [(i, i + 2) for i in range(frames - 2)]
    swap = [(i, i ^ 1) for i in range(frames)]
    main2 = lax.ppermute(main, "tm", later)
    if halos == 1:
        sides = [(near[0], [(0, 1), (1, 0)])]
    else:
        sides = [
            (near[1], [(j, j + 1) for j in range(tiles - 1)]),
            (near[0], [(j + 1, j) for j in range(tiles - 1)]),
        ]
    edges = [lax.ppermute(row, "tile", route) for row, route in sides]
    edges2 = [
        lax.ppermute(
            row,
            ("tm", "tile"),
            [(a * tiles + i, b * tiles + j) for a, b in later for i, j in route],
        )
        for row, route in sides
    ]
    stacked = lambda parts: parts[0] if len(parts) == 1 else jnp.concatenate(parts)
    edges, edges2 = stacked(edges), stacked(edges2)
    even = lax.ppermute(main2, "tm", swap), lax.ppermute(edges2, "tm", swap)
    odd = lax.ppermute(main, "tm", swap), lax.ppermute(edges, "tm", swap)
    return (main, edges), (main2, edges2), even + odd


def in_vmem(array):
    return pltpu.with_memory_space_constraint(array, pltpu.VMEM)


def local(latent, gain, conv_weight, conv_bias, time_weight, time_bias, up_weight, up_bias):
    tiles = lax.axis_size("tile")
    tile = lax.axis_index("tile")
    core = lax.axis_index("tm") % 2
    halos = 1 if tiles == 2 else 2
    main = latent[0]
    rows, cols, chans = main.shape
    outs_n = up_weight.shape[3]
    flip = tile if halos == 1 else 0 * tile
    place = jnp.stack([flip, tile > 0, tile < tiles - 1, core]).astype(jnp.int32)
    params = pltpu.CompilerParams(vmem_limit_bytes=20 << 20)
    field = jax.ShapeDtypeStruct((rows, cols, chans), BF16)
    sides = jax.ShapeDtypeStruct((halos, cols, chans), BF16)
    act = pltpu.VMEM((rows + halos, cols, chans), BF16)
    flops = 18 * rows * cols * chans * chans

    def cost(share):
        return pl.CostEstimate(flops=int(flops * share), bytes_accessed=1000000, transcendentals=0)

    def vmem(shape, dtype):
        return pltpu.VMEM(shape, dtype)

    merged = pl.pallas_call(
        merge_kernel,
        out_shape=vmem((2, 2 * chans, 4 * outs_n), BF16),
        in_specs=[SMEM, VMEM],
        out_specs=VMEM,
        compiler_params=params,
        cost_estimate=cost(1),
        name="merge_taps",
    )(place, up_weight.transpose(0, 1, 3, 2))

    if halos == 1:
        near = [lax.dynamic_slice_in_dim(main, (rows - 1) * (1 - tile), 1, 0)]
    else:
        near = [main[:1], main[rows - 1 :]]

    gain, conv_bias, time_bias, up_bias = gain[None], conv_bias[None], time_bias[None], up_bias[None]
    conv_weight = in_vmem(conv_weight)
    time_weight = in_vmem(time_weight.reshape(3 * chans, 2 * chans))
    frame, frame2, frame1 = exchange(main, near, halos)
    total = vmem((rows, cols, chans), F32)
    acc = pl.pallas_call(
        functools.partial(conv_first, halos),
        out_shape=total,
        in_specs=[SMEM] + [VMEM] * 5,
        out_specs=VMEM,
        scratch_shapes=[act],
        compiler_params=params,
        cost_estimate=cost(1),
        name="conv_own_frame",
    )(place, *frame, gain, conv_bias, conv_weight)
    acc = pl.pallas_call(
        functools.partial(conv_second, halos),
        out_shape=total,
        in_specs=[SMEM] + [VMEM] * 5,
        out_specs=VMEM,
        scratch_shapes=[act],
        compiler_params=params,
        cost_estimate=cost(1),
        name="conv_two_back",
    )(place, *frame2, acc, gain, conv_weight)
    block, near = pl.pallas_call(
        functools.partial(conv_third, halos),
        out_shape=(field, sides),
        in_specs=[SMEM] + [VMEM] * 7,
        out_specs=(VMEM, VMEM),
        scratch_shapes=[act, pltpu.VMEM(field.shape, BF16), pltpu.VMEM(sides.shape, BF16)],
        compiler_params=params,
        cost_estimate=cost(1),
        name="conv_one_back",
    )(place, *frame1, acc, gain, conv_weight)

    frame, frame2, frame1 = exchange(block, [near[h : h + 1] for h in range(halos)], halos)
    out = pl.pallas_call(
        functools.partial(up_kernel, halos),
        out_shape=jax.ShapeDtypeStruct((2, 2 * rows, outs_n, 2 * cols), BF16),
        in_specs=[SMEM] + [VMEM] * 12,
        out_specs=ANY,
        scratch_shapes=[
            pltpu.VMEM(field.shape, BF16),
            pltpu.VMEM(sides.shape, BF16),
            pltpu.VMEM((2, rows + halos, cols, chans), BF16),
            pltpu.VMEM((2, 2, 2 * cols, 128), F32),
            pltpu.VMEM((2, 2 * rows, outs_n, 2 * cols), BF16),
            pltpu.SemaphoreType.DMA((2, 2 * rows)),
        ],
        compiler_params=params,
        cost_estimate=cost(2),
        name="time_and_up",
    )(place, *frame, *frame2, *frame1, time_bias, up_bias, time_weight, merged)
    return out.transpose(0, 1, 3, 2)


def solution(mesh):
    placed = (P("tm", "tile", None, None), P(), P(), P(), P(), P(), P(), P())
    return jax.shard_map(
        local, mesh=mesh, in_specs=placed, out_specs=P("tm", "tile", None, None), check_vma=False
    )
```

```python
import functools

import jax
import jax.numpy as jnp
from jax import lax
from jax.experimental import pallas as pl
from jax.experimental.pallas import tpu as pltpu
from jax.sharding import PartitionSpec as P

F32 = jnp.float32
BF16 = jnp.bfloat16
VMEM = pl.BlockSpec(memory_space=pltpu.VMEM)
SMEM = pl.BlockSpec(memory_space=pltpu.SMEM)
ANY = pl.BlockSpec(memory_space=pl.ANY)
HBM = pl.BlockSpec(memory_space=pltpu.HBM)
LANES = 128
SHARE = 3000000000


def in_order(place, index, count):
    return jnp.where(place[0] == 1, count - 1 - index, index)


def activate(rows, gain):
    values = rows.astype(F32)
    meansq = jnp.mean(values * values, axis=-1, keepdims=True)
    scaled = values * lax.rsqrt(meansq + 1e-06) * gain
    return (scaled * jax.nn.sigmoid(scaled)).astype(BF16)


def moved(rows, step):
    cols = rows.shape[0]
    index = lax.broadcasted_iota(jnp.int32, rows.shape, 0)
    edge = 0 if step == 1 else cols - 1
    return jnp.where(index == edge, 0.0, pltpu.roll(rows, step % cols, 0))


def conv_rows(place, halos, rows, sources):
    lead = halos - 1
    sums = []
    for q in range(rows):
        lefts, rights = [], []
        for weight, field in sources:
            for dh in range(3):
                s = lead + q + dh - 1
                if s in field:
                    lefts.append(field[s]())
                    tap = in_order(place, dh, 3)
                    rights.append(jnp.concatenate([weight[tap, dw] for dw in range(3)], axis=-1))
        if not lefts:
            sums.append(None)
            continue
        total = jnp.dot(
            jnp.concatenate(lefts, axis=-1), jnp.concatenate(rights, axis=0), preferred_element_type=F32
        )
        chans = total.shape[1] // 3
        sums.append(
            total[:, chans : 2 * chans]
            + moved(total[:, :chans], 1)
            + moved(total[:, 2 * chans :], -1)
        )
    return sums


def hold(act, slot, value):
    act[slot] = value
    return lambda: act[slot]


def held_rows(place, halos, main, gain, act):
    rows = main.shape[0]
    return {
        halos - 1 + q: hold(act, q, activate(main[in_order(place, q, rows)], gain)) for q in range(rows)
    }


def held_edges(halos, rows, edges, gain, act, slot, known=True):
    where = (rows,) if halos == 1 else (0, rows + 1)
    return {
        s: hold(act, slot + h, activate(jnp.where(known, edges[h], jnp.zeros_like(edges[h])), gain))
        for h, s in enumerate(where)
    }


def loads(w_hbm, w, sems, dt):
    return [
        pltpu.make_async_copy(w_hbm.at[dt, dh, dw], w.at[dh, dw], sems.at[dh, dw])
        for dh in range(3)
        for dw in range(3)
    ]


def near_row(place, field, row):
    row[0] = field[in_order(place, field.shape[0] - 1, field.shape[0])]


def conv_first(halos, place, own, edges, gain, bias, w_hbm, acc, w0, w1, w2, act, sems):
    rows = own.shape[0]
    now = loads(w_hbm, w2, sems.at[2], 2)
    ahead = loads(w_hbm, w0, sems.at[0], 0) + loads(w_hbm, w1, sems.at[1], 1)
    for copy in now + ahead:
        copy.start()
    field = held_rows(place, halos, own, gain[...][None], act)
    field.update(held_edges(halos, rows, edges, gain[...][None], act, rows))
    for copy in now:
        copy.wait()
    for q, part in enumerate(conv_rows(place, halos, rows, [(w2, field)])):
        acc[q] = part + bias[...][None] + own[in_order(place, q, rows)].astype(F32)
    for copy in ahead:
        copy.wait()


def conv_second(halos, place, main, before, gain, w0, acc, act):
    rows = main.shape[0]

    @pl.when(place[4] == 0)
    def _():
        acc[...] = before[...]

    @pl.when(place[4] != 0)
    def _():
        field = held_rows(place, halos, main, gain[...][None], act)
        for q, part in enumerate(conv_rows(place, halos, rows, [(w0, field)])):
            acc[q] = before[q] + part


def pick(place, even, odd, chosen):
    @pl.when((place[3] == 0) & (place[4] == 0))
    def _():
        chosen[...] = jnp.zeros_like(chosen)

    @pl.when((place[3] == 0) & (place[4] != 0))
    def _():
        chosen[...] = even[...]

    @pl.when(place[3] != 0)
    def _():
        chosen[...] = odd[...]


def conv_third(halos, place, main_a, main_b, edges2, edges_a, edges_b, before, gain, w0, w1,
               block, near, act, main, edges):
    rows = block.shape[0]
    pick(place, main_a, main_b, main)
    pick(place, edges_a, edges_b, edges)
    field = held_rows(place, halos, main, gain[...][None], act)
    field.update(held_edges(halos, rows, edges, gain[...][None], act, rows))
    field2 = held_edges(halos, rows, edges2, gain[...][None], act, rows + halos, place[4] != 0)
    for q, part in enumerate(conv_rows(place, halos, rows, [(w1, field), (w0, field2)])):
        value = (before[q] + part).astype(BF16)
        block[in_order(place, q, rows)] = value
        if q == rows - 1:
            near[halos - 1] = value
        if q == 0 and halos == 2:
            near[0] = value


def up_rows(place, rows, out_rows, pairs, ubias, uw, wide, outs, out_hbm, osems):
    cols = wide.shape[2] // 2
    rest = ubias.shape[-1] - LANES
    chans = uw.shape[1] // 2
    lane = lax.broadcasted_iota(jnp.int32, (cols, LANES), 1)
    stores = []
    for slot_o, o in enumerate(out_rows):
        phase, taken = pairs[o]
        left = jnp.concatenate([jnp.concatenate([r[f] for r in taken], axis=-1) for f in range(2)], axis=0)
        right = uw[phase, (2 - len(taken)) * chans :, :]
        both = jnp.dot(left, right, preferred_element_type=F32)
        for f in range(2):
            part = both[f * cols : (f + 1) * cols]
            g = [part[:, k * LANES : (k + 1) * LANES] for k in range(6)]
            tail = g[4] + jnp.where(lane < rest, moved(g[5], 1), moved(g[5], -1))
            slot = f
            wide[slot, 0, pl.ds(0, cols, stride=2), :] = g[0] + moved(g[2], 1) + ubias[:LANES][None]
            wide[slot, 0, pl.ds(1, cols, stride=2), :] = g[1] + moved(g[3], -1) + ubias[:LANES][None]
            wide[slot, 1, pl.ds(0, cols, stride=2), :] = tail
            wide[slot, 1, pl.ds(1, cols, stride=2), :] = pltpu.roll(tail, LANES - rest, 1)
            outs[f, slot_o, :LANES, :] = wide[slot, 0].T.astype(BF16)
            outs[f, slot_o, LANES:, :] = (wide[slot, 1, :, :rest] + ubias[LANES:][None]).T.astype(BF16)
            copy = pltpu.make_async_copy(
                outs.at[f, slot_o], out_hbm.at[f, in_order(place, o, 2 * rows)], osems.at[f, slot_o]
            )
            copy.start()
            stores.append(copy)
    return stores


def inner_rows(halos, rows):
    inner = list(range(0 if halos == 1 else 1, 2 * rows - 1))
    return inner, [o for o in range(2 * rows) if o not in inner]


def up_main(halos, place, own, main2, main_a, main_b, tbias, ubias, tw, uw,
            out_hbm, kept, main1, doubled, wide, outs, osems):
    rows, cols, chans = own.shape
    pick(place, main_a, main_b, main1)
    lefts = []
    for q in range(rows):
        at = in_order(place, q, rows)
        first = main2[at]
        first = jnp.where(place[4] != 0, first, jnp.zeros_like(first))
        lefts.append(jnp.concatenate([first, main1[at], own[at]], axis=-1))
    mixed = jnp.dot(jnp.concatenate(lefts, axis=0), tw[...], preferred_element_type=F32) + tbias[...][None]
    for q in range(rows):
        for f in range(2):
            value = mixed[q * cols : (q + 1) * cols, f * chans : (f + 1) * chans].astype(BF16)
            doubled[f, q] = value
            if q == rows - 1:
                kept[f, halos - 1] = value
            if q == 0 and halos == 2:
                kept[f, 0] = value

    pairs = {}
    for q in range(rows):
        for phase in range(2):
            sources = [s for s in (q - 1 + phase, q + phase) if 0 <= s < rows]
            pairs[2 * q + phase] = phase, [[doubled[f, s] for f in range(2)] for s in sources]
    out_rows = inner_rows(halos, rows)[0]
    for copy in up_rows(place, rows, out_rows, pairs, ubias, uw, wide, outs, out_hbm, osems):
        copy.wait()


def up_edge(halos, place, edges, edges2, edges_a, edges_b, kept, tbias, ubias, tw, uw, out_so_far,
            out_hbm, edges1, doubled, wide, outs, osems):
    del out_so_far
    cols, chans = edges.shape[1:]
    rows = out_hbm.shape[1] // 2
    pick(place, edges_a, edges_b, edges1)
    first = [jnp.where(place[4] != 0, edges2[h], jnp.zeros_like(edges2[h])) for h in range(halos)]
    left = jnp.concatenate(
        [jnp.concatenate([first[h], edges1[h], edges[h]], axis=-1) for h in range(halos)], axis=0
    )
    mixed = jnp.dot(left, tw[...], preferred_element_type=F32) + tbias[...][None]
    for h in range(halos):
        value = mixed[h * cols : (h + 1) * cols]
        if halos == 2:
            value = jnp.where(place[1 + h] == 1, value, 0.0)
        for f in range(2):
            doubled[f, h] = value[:, f * chans : (f + 1) * chans].astype(BF16)
    last = halos - 1
    pairs = {2 * rows - 1: (1, [[kept[f, last] for f in range(2)], [doubled[f, last] for f in range(2)]])}
    if halos == 2:
        pairs[0] = (0, [[doubled[f, 0] for f in range(2)], [kept[f, 0] for f in range(2)]])
    out_rows = inner_rows(halos, rows)[1]
    for copy in up_rows(place, rows, out_rows, pairs, ubias, uw, wide, outs, out_hbm, osems):
        copy.wait()


def merge_kernel(place, taps_hbm, tw_hbm, merged, tw, taps, sems):
    load = pltpu.make_async_copy(taps_hbm, taps, sems.at[0])
    load.start()
    copy = pltpu.make_async_copy(tw_hbm, tw, sems.at[1])
    copy.start()
    load.wait()
    chans = taps.shape[3]

    def tap(dh, dw):
        return taps[in_order(place, dh, 3), dw].astype(F32)

    for phase, sets in enumerate((((0,), (1, 2)), ((0, 1), (2,)))):
        for which, rows in enumerate(sets):
            cols = [sum(tap(dh, dw) for dh in rows) for dw in range(3)]
            groups = (cols[1] + cols[2], cols[0] + cols[1], cols[0], cols[2])
            wide = jnp.concatenate([g[:LANES] for g in groups] + [g[LANES:] for g in groups], axis=0)
            merged[phase, which * chans : (which + 1) * chans, :] = wide.T.astype(BF16)
    copy.wait()


def in_hbm(array):
    return pltpu.with_memory_space_constraint(array, pltpu.HBM)


def after(array, *others):
    return lax.optimization_barrier((array, *others))[0]


def in_chip(array):
    return lax.ppermute(array, "tm", [(i, i ^ 1) for i in range(lax.axis_size("tm"))])


def two_back(array):
    frames = lax.axis_size("tm")
    return lax.ppermute(array, "tm", [(i, (i + 2) % frames) for i in range(frames)])


def beside(near, halos):
    frames = lax.axis_size("tm")
    tiles = lax.axis_size("tile")
    if halos == 1:
        sides = [(near[0], [(0, 1), (1, 0)])]
    else:
        sides = [
            (near[1], [(j, j + 1) for j in range(tiles - 1)]),
            (near[0], [(j + 1, j) for j in range(tiles - 1)]),
        ]
    edges2 = [
        lax.ppermute(
            row,
            ("tm", "tile"),
            [(a * tiles + i, (a + 2) % frames * tiles + j) for a in range(frames) for i, j in route],
        )
        for row, route in sides
    ]
    edges = [lax.ppermute(row, "tile", route) for row, route in sides]
    if halos == 1:
        return edges[0], edges2[0]
    return jnp.concatenate(edges), jnp.concatenate(edges2)


def local(latent, gain, conv_weight, conv_bias, time_weight, time_bias, up_weight, up_bias):
    tiles = lax.axis_size("tile")
    tile = lax.axis_index("tile")
    frame_at = lax.axis_index("tm")
    halos = 1 if tiles == 2 else 2
    main = latent[0]
    rows, cols, chans = main.shape
    outs_n = up_weight.shape[3]
    flip = tile if halos == 1 else 0 * tile
    place = jnp.stack([flip, tile > 0, tile < tiles - 1, frame_at % 2, frame_at >= 2]).astype(jnp.int32)

    def call(kernel, name, share, ins, outs, scratch, **rest):
        return pl.pallas_call(
            kernel,
            out_shape=tuple(s for s, _ in outs),
            in_specs=[SMEM] + ins,
            out_specs=tuple(s for _, s in outs),
            scratch_shapes=scratch,
            compiler_params=pltpu.CompilerParams(vmem_limit_bytes=20 << 20),
            cost_estimate=pl.CostEstimate(
                flops=int(SHARE * share), bytes_accessed=1000, transcendentals=0
            ),
            name=name,
            **rest,
        )

    field = (rows, cols, chans)
    sides = (halos, cols, chans)
    taps = pltpu.VMEM((3, 3, chans, chans), BF16)
    total = (pltpu.VMEM(field, F32), VMEM)
    taps_t = in_hbm(up_weight.transpose(0, 1, 3, 2))
    merge = call(
        merge_kernel, "merge_taps", 1,
        [HBM, HBM],
        [(pltpu.VMEM((2, 2 * chans, 4 * outs_n), BF16), VMEM), (pltpu.VMEM((3 * chans, 2 * chans), BF16), VMEM)],
        [pltpu.VMEM((3, 3, outs_n, chans), BF16), pltpu.SemaphoreType.DMA((2,))],
    )

    if halos == 1:
        near = call(near_row, "near_row", 3, [VMEM], [(jax.ShapeDtypeStruct(sides, BF16), VMEM)], [])(place, main)
    else:
        near = [main[:1], main[rows - 1 :]]
    main2 = two_back(main)
    edges, edges2 = beside(near, halos)
    odd = in_chip(main)
    even = in_chip(main2)
    acc, w0, w1 = call(
        functools.partial(conv_first, halos), "conv_own_frame", 0.2,
        [VMEM] * 4 + [HBM],
        [total, (taps, VMEM), (taps, VMEM)],
        [taps, pltpu.VMEM((rows + halos, cols, chans), BF16), pltpu.SemaphoreType.DMA((3, 3, 3))],
    )(place, main, edges, gain, conv_bias, in_hbm(conv_weight))
    odd_edges = in_chip(edges)
    own_acc = acc
    (acc,) = call(
        functools.partial(conv_second, halos), "conv_two_back", 1,
        [VMEM] * 4,
        [total],
        [pltpu.VMEM(field, BF16)],
    )(place, main2, acc, gain, w0)
    even_edges = in_chip(after(edges2, own_acc))
    block, near = call(
        functools.partial(conv_third, halos), "conv_one_back", 1,
        [VMEM] * 9,
        [(jax.ShapeDtypeStruct(field, BF16), VMEM), (jax.ShapeDtypeStruct(sides, BF16), VMEM)],
        [
            pltpu.VMEM((rows + 2 * halos, cols, chans), BF16),
            pltpu.VMEM(field, BF16),
            pltpu.VMEM(sides, BF16),
        ],
    )(place, even, odd, edges2, even_edges, odd_edges, acc, gain, w0, w1)

    near = [near[h : h + 1] for h in range(halos)]
    main = block
    main2 = two_back(main)
    edges, edges2 = beside(near, halos)
    odd = in_chip(main)
    merged, tw = merge(place, after(taps_t, block), in_hbm(time_weight.reshape(3 * chans, 2 * chans)))
    even = in_chip(main2)
    mains = main, main2, even, odd
    edges = edges, edges2, in_chip(after(edges2, merged)), in_chip(edges)
    inner, outer = (len(o) for o in inner_rows(halos, rows))
    out_shape = (jax.ShapeDtypeStruct((2, 2 * rows, outs_n, 2 * cols), BF16), ANY)

    def scratch(count, held):
        return [
            pltpu.VMEM((2, held, cols, chans), BF16),
            pltpu.VMEM((2, 2, 2 * cols, LANES), F32),
            pltpu.VMEM((2, count, outs_n, 2 * cols), BF16),
            pltpu.SemaphoreType.DMA((2, count)),
        ]

    out, kept = call(
        functools.partial(up_main, halos), "time_and_up", 2,
        [VMEM] * 8,
        [out_shape, (pltpu.VMEM((2,) + sides, BF16), VMEM)],
        [pltpu.VMEM(field, BF16)] + scratch(inner, rows),
    )(place, *mains, time_bias, up_bias, tw, merged)
    (out,) = call(
        functools.partial(up_edge, halos), "time_and_up_edge", 1,
        [VMEM] * 9 + [ANY],
        [out_shape],
        [pltpu.VMEM(sides, BF16)] + scratch(outer, halos),
        input_output_aliases={10: 0},
    )(place, *edges, kept, time_bias, up_bias, tw, merged, out)
    return out.transpose(0, 1, 3, 2)


def solution(mesh):
    placed = (P("tm", "tile", None, None), P(), P(), P(), P(), P(), P(), P())
    return jax.shard_map(
        local, mesh=mesh, in_specs=placed, out_specs=P("tm", "tile", None, None), check_vma=False
    )
```

```python
import functools

import jax
import jax.numpy as jnp
from jax import lax
from jax.experimental import pallas as pl
from jax.experimental.pallas import tpu as pltpu
from jax.sharding import PartitionSpec as P

F32 = jnp.float32
BF16 = jnp.bfloat16
VMEM = pl.BlockSpec(memory_space=pltpu.VMEM)
SMEM = pl.BlockSpec(memory_space=pltpu.SMEM)
ANY = pl.BlockSpec(memory_space=pl.ANY)
HBM = pl.BlockSpec(memory_space=pltpu.HBM)
LANES = 128
SHARE = 3000000000
SPLIT = 1
OWN = 0.2
TWO = 0.2
THREE = 1
MERGE = 0.2
FIRST = 0.01


def in_order(place, index, count):
    return jnp.where(place[0] == 1, count - 1 - index, index)


def activate(rows, gain):
    values = rows.astype(F32)
    meansq = jnp.mean(values * values, axis=-1, keepdims=True)
    scaled = values * lax.rsqrt(meansq + 1e-06) * gain
    return (scaled * jax.nn.sigmoid(scaled)).astype(BF16)


def moved(rows, step):
    cols = rows.shape[0]
    index = lax.broadcasted_iota(jnp.int32, rows.shape, 0)
    edge = 0 if step == 1 else cols - 1
    return jnp.where(index == edge, 0.0, pltpu.roll(rows, step % cols, 0))


def conv_rows(place, halos, rows, sources):
    lead = halos - 1
    sums = []
    for q in range(rows):
        lefts, rights = [], []
        for weight, field in sources:
            for dh in range(3):
                s = lead + q + dh - 1
                if s in field:
                    lefts.append(field[s]())
                    tap = in_order(place, dh, 3)
                    rights.append(jnp.concatenate([weight[tap, dw] for dw in range(3)], axis=-1))
        if not lefts:
            sums.append(None)
            continue
        total = jnp.dot(
            jnp.concatenate(lefts, axis=-1), jnp.concatenate(rights, axis=0), preferred_element_type=F32
        )
        chans = total.shape[1] // 3
        sums.append(
            total[:, chans : 2 * chans]
            + moved(total[:, :chans], 1)
            + moved(total[:, 2 * chans :], -1)
        )
    return sums


def hold(act, slot, value):
    act[slot] = value
    return lambda: act[slot]


def parts_row(halos, rows, near, rest, q):
    if halos == 1:
        return near[0] if q == rows - 1 else rest[q]
    if q in (0, rows - 1):
        return near[0 if q == 0 else 1]
    return rest[q - 1]


def held_rows(halos, rows, row, gain, act):
    return {halos - 1 + q: hold(act, q, activate(row(q), gain)) for q in range(rows)}


def held_edges(halos, rows, edges, gain, act, slot, known=True):
    where = (rows,) if halos == 1 else (0, rows + 1)
    return {
        s: hold(act, slot + h, activate(jnp.where(known, edges[h], jnp.zeros_like(edges[h])), gain))
        for h, s in enumerate(where)
    }


def split_rows(halos, place, field, near, rest):
    rows = field.shape[0]
    if halos == 2:
        near[0] = field[0]
    near[halos - 1] = field[in_order(place, rows - 1, rows)]
    for i in range(rows - halos):
        rest[i] = field[in_order(place, halos - 1 + i, rows)]


def conv_first(halos, place, own, gain, bias, weight, acc, act):
    rows = own.shape[0]
    row = lambda q: own[in_order(place, q, rows)]
    field = held_rows(halos, rows, row, gain[...][None], act)
    for q, part in enumerate(conv_rows(place, halos, rows, [(weight.at[2], field)])):
        acc[q] = part + bias[...][None] + row(q).astype(F32)


def conv_second(halos, place, near2, rest2, before, gain, weight, acc, act):
    rows = before.shape[0]

    @pl.when(place[4] == 0)
    def _():
        acc[...] = before[...]

    @pl.when(place[4] != 0)
    def _():
        row = lambda q: parts_row(halos, rows, near2, rest2, q)
        field = held_rows(halos, rows, row, gain[...][None], act)
        for q, part in enumerate(conv_rows(place, halos, rows, [(weight.at[0], field)])):
            acc[q] = before[q] + part


def one_back(place, even, odd):
    none = jnp.zeros_like(odd)
    return jnp.where(place[3] != 0, odd, jnp.where(place[4] != 0, even, none))


def conv_third(halos, place, even_near, even_rest, odd, before, gain, weight, acc, act):
    rows = before.shape[0]

    def row(q):
        return one_back(place, parts_row(halos, rows, even_near, even_rest, q), odd[in_order(place, q, rows)])

    field = held_rows(halos, rows, row, gain[...][None], act)
    for q, part in enumerate(conv_rows(place, halos, rows, [(weight.at[1], field)])):
        acc[q] = before[q] + part


def conv_edges(halos, place, edges, edges2, even_edges, odd_edges, before, gain, weight, block, near, rest, act):
    rows = block.shape[0]
    sides = [one_back(place, even_edges[h], odd_edges[h]) for h in range(halos)]
    fields = [
        (weight.at[dt], held_edges(halos, rows, field, gain[...][None], act, dt * halos, known))
        for dt, field, known in ((2, edges, True), (1, sides, True), (0, edges2, place[4] != 0))
    ]
    for q, part in enumerate(conv_rows(place, halos, rows, fields)):
        value = (before[q] if part is None else before[q] + part).astype(BF16)
        block[in_order(place, q, rows)] = value
        if q == rows - 1:
            near[halos - 1] = value
        elif q == 0 and halos == 2:
            near[0] = value
        else:
            rest[q - (halos - 1)] = value


def up_rows(place, rows, out_rows, pairs, ubias, uw, wide, outs, out_hbm, osems):
    cols = wide.shape[2] // 2
    rest = ubias.shape[-1] - LANES
    chans = uw.shape[1] // 2
    lane = lax.broadcasted_iota(jnp.int32, (cols, LANES), 1)
    stores = []
    for slot_o, o in enumerate(out_rows):
        phase, taken = pairs[o]
        left = jnp.concatenate([jnp.concatenate([r[f] for r in taken], axis=-1) for f in range(2)], axis=0)
        right = uw[phase, (2 - len(taken)) * chans :, :]
        both = jnp.dot(left, right, preferred_element_type=F32)
        for f in range(2):
            part = both[f * cols : (f + 1) * cols]
            g = [part[:, k * LANES : (k + 1) * LANES] for k in range(6)]
            tail = g[4] + jnp.where(lane < rest, moved(g[5], 1), moved(g[5], -1))
            slot = f
            wide[slot, 0, pl.ds(0, cols, stride=2), :] = g[0] + moved(g[2], 1) + ubias[:LANES][None]
            wide[slot, 0, pl.ds(1, cols, stride=2), :] = g[1] + moved(g[3], -1) + ubias[:LANES][None]
            wide[slot, 1, pl.ds(0, cols, stride=2), :] = tail
            wide[slot, 1, pl.ds(1, cols, stride=2), :] = pltpu.roll(tail, LANES - rest, 1)
            outs[f, slot_o, :LANES, :] = wide[slot, 0].T.astype(BF16)
            outs[f, slot_o, LANES:, :] = (wide[slot, 1, :, :rest] + ubias[LANES:][None]).T.astype(BF16)
            copy = pltpu.make_async_copy(
                outs.at[f, slot_o], out_hbm.at[f, in_order(place, o, 2 * rows)], osems.at[f, slot_o]
            )
            copy.start()
            stores.append(copy)
    return stores


def doubled_rows(lefts, tw, tbias, keep):
    cols = lefts[0].shape[0]
    chans = tw.shape[1] // 2
    mixed = jnp.dot(jnp.concatenate(lefts, axis=0), tw[...], preferred_element_type=F32) + tbias[...][None]
    for i in range(len(lefts)):
        for f in range(2):
            keep(i, f, mixed[i * cols : (i + 1) * cols, f * chans : (f + 1) * chans])


def inside(place, halos, h, value):
    return jnp.where(place[1 + h] == 1, value, 0.0) if halos == 2 else value


def row_pairs(halos, rows, at, out_rows):
    lead = halos - 1
    pairs = {}
    for o in out_rows:
        q, phase = divmod(o, 2)
        sources = [s for s in (lead + q - 1 + phase, lead + q + phase) if s >= 0]
        pairs[o] = phase, [[at(s, f) for f in range(2)] for s in sources]
    return pairs


def inner_rows(halos, rows):
    inner = list(range(0 if halos == 1 else 1, 2 * rows - 1))
    return inner, [o for o in range(2 * rows) if o not in inner]


def first_inner(halos, place, own, odd, tbias, ubias, tw, uw, out_hbm, kept, doubled, wide, outs, osems):
    @pl.when(place[4] == 0)
    def _():
        rows = own.shape[0]
        lead = halos - 1
        lefts = []
        for q in range(rows):
            now, before = own[in_order(place, q, rows)], odd[in_order(place, q, rows)]
            none = jnp.zeros_like(now)
            lefts.append(jnp.concatenate([none, jnp.where(place[3] == 0, none, before), now], axis=-1))

        def keep(q, f, value):
            value = value.astype(BF16)
            doubled[f, q] = value
            if q == rows - 1:
                kept[f, halos - 1] = value
            elif q == 0 and halos == 2:
                kept[f, 0] = value

        doubled_rows(lefts, tw, tbias, keep)
        out_rows = inner_rows(halos, rows)[0]
        pairs = row_pairs(halos, rows, lambda s, f: doubled[f, s - lead], out_rows)
        for copy in up_rows(place, rows, out_rows, pairs, ubias, uw, wide, outs, out_hbm, osems):
            copy.wait()


def first_edges(halos, place, edges, odd_edges, kept, tbias, ubias, tw, uw, out_so_far,
                out_hbm, token, doubled, wide, outs, osems):
    del out_so_far
    token[...] = jnp.zeros_like(token)

    @pl.when(place[4] == 0)
    def _():
        rows = out_hbm.shape[1] // 2
        lead = halos - 1
        lefts = []
        for h in range(halos):
            none = jnp.zeros_like(edges[h])
            lefts.append(jnp.concatenate([none, jnp.where(place[3] == 0, none, odd_edges[h]), edges[h]], axis=-1))

        def keep(h, f, value):
            doubled[f, h] = inside(place, halos, h, value).astype(BF16)

        doubled_rows(lefts, tw, tbias, keep)

        def at(s, f):
            if lead <= s < lead + rows:
                return kept[f, 0 if s == lead and halos == 2 else halos - 1]
            return doubled[f, 0 if s < lead else halos - 1]

        out_rows = inner_rows(halos, rows)[1]
        pairs = row_pairs(halos, rows, at, out_rows)
        for copy in up_rows(place, rows, out_rows, pairs, ubias, uw, wide, outs, out_hbm, osems):
            copy.wait()


def up_kernel(halos, place, own, near2, rest2, even_near, even_rest, odd, edges, edges2, even_edges, odd_edges,
              tbias, ubias, tw, uw, token, out_so_far, out_hbm, doubled, wide, outs, osems):
    del token, out_so_far

    @pl.when(place[4] != 0)
    def _():
        rows = own.shape[0]
        lead = halos - 1
        lefts = []
        for s in range(rows + halos):
            if lead <= s < lead + rows:
                q = s - lead
                now, mine = own[in_order(place, q, rows)], odd[in_order(place, q, rows)]
                theirs = parts_row(halos, rows, even_near, even_rest, q)
                first = parts_row(halos, rows, near2, rest2, q)
            else:
                h = 0 if s < lead else halos - 1
                now, mine, theirs, first = edges[h], odd_edges[h], even_edges[h], edges2[h]
            lefts.append(jnp.concatenate([first, jnp.where(place[3] == 0, theirs, mine), now], axis=-1))

        def keep(s, f, value):
            if not lead <= s < lead + rows:
                value = inside(place, halos, 0 if s < lead else halos - 1, value)
            doubled[f, s] = value.astype(BF16)

        doubled_rows(lefts, tw, tbias, keep)
        out_rows = range(2 * rows)
        pairs = row_pairs(halos, rows, lambda s, f: doubled[f, s], out_rows)
        for copy in up_rows(place, rows, out_rows, pairs, ubias, uw, wide, outs, out_hbm, osems):
            copy.wait()


def merge_kernel(place, taps, merged):
    chans = taps.shape[3]

    def tap(dh, dw):
        return taps[in_order(place, dh, 3), dw].astype(F32)

    for phase, sets in enumerate((((0,), (1, 2)), ((0, 1), (2,)))):
        for which, rows in enumerate(sets):
            cols = [sum(tap(dh, dw) for dh in rows) for dw in range(3)]
            groups = (cols[1] + cols[2], cols[0] + cols[1], cols[0], cols[2])
            wide = jnp.concatenate([g[:LANES] for g in groups] + [g[LANES:] for g in groups], axis=0)
            merged[phase, which * chans : (which + 1) * chans, :] = wide.T.astype(BF16)


def in_hbm(array):
    return pltpu.with_memory_space_constraint(array, pltpu.HBM)


def together(*arrays):
    return lax.optimization_barrier(arrays)


def in_chip(array):
    return lax.ppermute(array, "tm", [(i, i ^ 1) for i in range(lax.axis_size("tm"))])


def two_back(array):
    frames = lax.axis_size("tm")
    return lax.ppermute(array, "tm", [(i, (i + 2) % frames) for i in range(frames)])


def beside(near):
    tiles = lax.axis_size("tile")
    if tiles == 2:
        return lax.ppermute(near, "tile", [(0, 1), (1, 0)])
    return jnp.concatenate(
        [
            lax.ppermute(near[1:], "tile", [(j, j + 1) for j in range(tiles - 1)]),
            lax.ppermute(near[:1], "tile", [(j + 1, j) for j in range(tiles - 1)]),
        ]
    )


def local(latent, gain, conv_weight, conv_bias, time_weight, time_bias, up_weight, up_bias):
    tiles = lax.axis_size("tile")
    tile = lax.axis_index("tile")
    frame_at = lax.axis_index("tm")
    halos = 1 if tiles == 2 else 2
    main = latent[0]
    rows, cols, chans = main.shape
    outs_n = up_weight.shape[3]
    flip = tile if halos == 1 else 0 * tile
    place = jnp.stack([flip, tile > 0, tile < tiles - 1, frame_at % 2, frame_at >= 2]).astype(jnp.int32)

    def call(kernel, name, share, ins, outs, scratch, **rest):
        return pl.pallas_call(
            kernel,
            out_shape=tuple(s for s, _ in outs),
            in_specs=[SMEM] + ins,
            out_specs=tuple(s for _, s in outs),
            scratch_shapes=scratch,
            compiler_params=pltpu.CompilerParams(vmem_limit_bytes=20 << 20),
            cost_estimate=pl.CostEstimate(
                flops=int(SHARE * share), bytes_accessed=1000, transcendentals=0
            ),
            name=name,
            **rest,
        )

    field = (rows, cols, chans)
    sides = (halos, cols, chans)

    def conv(kernel, name, share, count):
        step = call(
            functools.partial(kernel, halos), name, share,
            [VMEM] * count,
            [(pltpu.VMEM(field, F32), VMEM)],
            [pltpu.VMEM(field, BF16)],
        )
        return lambda *arrays: step(*arrays)[0]

    taps_t = up_weight.transpose(0, 1, 3, 2)
    merge = call(
        merge_kernel, "merge_taps", MERGE,
        [VMEM],
        [(pltpu.VMEM((2, 2 * chans, 4 * outs_n), BF16), VMEM)],
        [],
    )
    near_rest = [
        (jax.ShapeDtypeStruct(sides, BF16), VMEM),
        (jax.ShapeDtypeStruct((max(rows - halos, 1), cols, chans), BF16), VMEM),
    ]
    if rows == halos:
        other = lambda near, rest, move: near
    else:
        other = lambda near, rest, move: move(rest)

    near, rest = call(functools.partial(split_rows, halos), "split_rows", SPLIT, [VMEM], near_rest, [])(place, main)
    near2 = two_back(near)
    edges = beside(near)
    odd = in_chip(main)
    rest2 = other(near2, rest, two_back)
    edges2 = beside(near2)
    even_near = in_chip(near2)
    acc = conv(conv_first, "conv_own_frame", OWN, 4)(place, main, gain, conv_bias, conv_weight)
    rest2, acc = together(rest2, acc)
    even_rest = other(even_near, rest2, in_chip)
    odd_edges = in_chip(edges)
    acc = conv(conv_second, "conv_two_back", TWO, 5)(place, near2, rest2, acc, gain, conv_weight)
    edges2, acc = together(edges2, acc)
    even_edges = in_chip(edges2)
    acc = conv(conv_third, "conv_one_back", THREE, 6)(place, even_near, even_rest, odd, acc, gain, conv_weight)
    block, near, rest = call(
        functools.partial(conv_edges, halos), "conv_edge_rows", 1,
        [VMEM] * 7,
        [(jax.ShapeDtypeStruct(field, BF16), VMEM)] + near_rest,
        [pltpu.VMEM((3 * halos, cols, chans), BF16)],
    )(place, edges, edges2, even_edges, odd_edges, acc, gain, conv_weight)

    near2 = two_back(near)
    edges = beside(near)
    odd = in_chip(block)
    taps_t, main = together(taps_t, block)
    (merged,) = merge(place, taps_t)
    tw = time_weight.reshape(3 * chans, 2 * chans)
    out_shape = (jax.ShapeDtypeStruct((2, 2 * rows, outs_n, 2 * cols), BF16), ANY)

    def scratch(count, held):
        return [
            pltpu.VMEM((2, held, cols, chans), BF16),
            pltpu.VMEM((2, 2, 2 * cols, LANES), F32),
            pltpu.VMEM((2, count, outs_n, 2 * cols), BF16),
            pltpu.SemaphoreType.DMA((2, count)),
        ]

    rest, merged = together(rest, merged)
    rest2 = other(near2, rest, two_back)
    common = (time_bias, up_bias, tw, merged)
    inner, outer = (len(o) for o in inner_rows(halos, rows))
    out, kept = call(
        functools.partial(first_inner, halos), "first_chip_inner_rows", FIRST,
        [VMEM] * 6,
        [out_shape, (pltpu.VMEM((2,) + sides, BF16), VMEM)],
        scratch(inner, rows),
    )(place, main, odd, *common)
    near2, kept = together(near2, kept)
    edges2 = beside(near2)
    even_near = in_chip(near2)
    odd_edges = in_chip(edges)
    out, token = call(
        functools.partial(first_edges, halos), "first_chip_edge_rows", FIRST,
        [VMEM] * 7 + [ANY],
        [out_shape, (jax.ShapeDtypeStruct((8, LANES), F32), VMEM)],
        scratch(outer, halos),
        input_output_aliases={8: 0},
    )(place, edges, odd_edges, kept, *common, out)
    rest2, token = together(rest2, token)
    even_rest = other(even_near, rest2, in_chip)
    even_edges = in_chip(edges2)
    (out,) = call(
        functools.partial(up_kernel, halos), "time_and_up", 1,
        [VMEM] * 14 + [ANY] * 2,
        [out_shape],
        scratch(2 * rows, rows + halos),
        input_output_aliases={16: 0},
    )(place, main, near2, rest2, even_near, even_rest, odd, edges, edges2, even_edges, odd_edges,
      *common, token, out)
    return out.transpose(0, 1, 3, 2)


def solution(mesh):
    placed = (P("tm", "tile", None, None), P(), P(), P(), P(), P(), P(), P())
    return jax.shard_map(
        local, mesh=mesh, in_specs=placed, out_specs=P("tm", "tile", None, None), check_vma=False
    )
```

```python
import functools

import jax
import jax.numpy as jnp
from jax import lax
from jax.experimental import pallas as pl
from jax.experimental.pallas import tpu as pltpu
from jax.sharding import PartitionSpec as P

F32 = jnp.float32
BF16 = jnp.bfloat16
VMEM = pl.BlockSpec(memory_space=pltpu.VMEM)
SMEM = pl.BlockSpec(memory_space=pltpu.SMEM)
ANY = pl.BlockSpec(memory_space=pl.ANY)
HBM = pl.BlockSpec(memory_space=pltpu.HBM)
LANES = 128
SHARE = 3000000000
SPLIT = 1
OWN = 0.2
TWO = 0.2
THREE = 1
MERGE = 0.2
FIRST = 0.01


def in_order(place, index, count):
    return jnp.where(place[0] == 1, count - 1 - index, index)


def activate(rows, gain):
    values = rows.astype(F32)
    meansq = jnp.mean(values * values, axis=-1, keepdims=True)
    scaled = values * lax.rsqrt(meansq + 1e-06) * gain
    return (scaled * jax.nn.sigmoid(scaled)).astype(BF16)


def moved(rows, step):
    cols = rows.shape[0]
    index = lax.broadcasted_iota(jnp.int32, rows.shape, 0)
    edge = 0 if step == 1 else cols - 1
    return jnp.where(index == edge, 0.0, pltpu.roll(rows, step % cols, 0))


def conv_rows(place, halos, rows, sources):
    lead = halos - 1
    sums = []
    for q in range(rows):
        lefts, rights = [], []
        for weight, field in sources:
            for dh in range(3):
                s = lead + q + dh - 1
                if s in field:
                    lefts.append(field[s]())
                    tap = in_order(place, dh, 3)
                    rights.append(jnp.concatenate([weight[tap, dw] for dw in range(3)], axis=-1))
        if not lefts:
            sums.append(None)
            continue
        total = jnp.dot(
            jnp.concatenate(lefts, axis=-1), jnp.concatenate(rights, axis=0), preferred_element_type=F32
        )
        chans = total.shape[1] // 3
        sums.append(
            total[:, chans : 2 * chans]
            + moved(total[:, :chans], 1)
            + moved(total[:, 2 * chans :], -1)
        )
    return sums


def hold(act, slot, value):
    act[slot] = value
    return lambda: act[slot]


def parts_row(halos, rows, near, rest, q):
    if halos == 1:
        return near[0] if q == rows - 1 else rest[q]
    if q in (0, rows - 1):
        return near[0 if q == 0 else 1]
    return rest[q - 1]


def held_rows(halos, rows, row, gain, act):
    return {halos - 1 + q: hold(act, q, activate(row(q), gain)) for q in range(rows)}


def held_edges(halos, rows, edges, gain, act, slot, known=True):
    where = (rows,) if halos == 1 else (0, rows + 1)
    return {
        s: hold(act, slot + h, activate(jnp.where(known, edges[h], jnp.zeros_like(edges[h])), gain))
        for h, s in enumerate(where)
    }


def split_rows(halos, place, field, near, rest):
    rows = field.shape[0]
    if halos == 2:
        near[0] = field[0]
    near[halos - 1] = field[in_order(place, rows - 1, rows)]
    for i in range(rows - halos):
        rest[i] = field[in_order(place, halos - 1 + i, rows)]


def conv_first(halos, place, own, gain, bias, weight, acc, act):
    rows = own.shape[0]
    row = lambda q: own[in_order(place, q, rows)]
    field = held_rows(halos, rows, row, gain[...][None], act)
    for q, part in enumerate(conv_rows(place, halos, rows, [(weight.at[2], field)])):
        acc[q] = part + bias[...][None] + row(q).astype(F32)


def conv_second(halos, place, near2, rest2, before, gain, weight, acc, act):
    rows = before.shape[0]

    @pl.when(place[4] == 0)
    def _():
        acc[...] = before[...]

    @pl.when(place[4] != 0)
    def _():
        row = lambda q: parts_row(halos, rows, near2, rest2, q)
        field = held_rows(halos, rows, row, gain[...][None], act)
        for q, part in enumerate(conv_rows(place, halos, rows, [(weight.at[0], field)])):
            acc[q] = before[q] + part


def one_back(place, even, odd):
    none = jnp.zeros_like(odd)
    return jnp.where(place[3] != 0, odd, jnp.where(place[4] != 0, even, none))


def conv_third(halos, place, even_near, even_rest, odd, before, gain, weight, acc, act):
    rows = before.shape[0]

    def row(q):
        return one_back(place, parts_row(halos, rows, even_near, even_rest, q), odd[in_order(place, q, rows)])

    field = held_rows(halos, rows, row, gain[...][None], act)
    for q, part in enumerate(conv_rows(place, halos, rows, [(weight.at[1], field)])):
        acc[q] = before[q] + part


def conv_edges(halos, place, edges, edges2, even_edges, odd_edges, before, gain, weight, block, near, rest, act):
    rows = block.shape[0]
    sides = [one_back(place, even_edges[h], odd_edges[h]) for h in range(halos)]
    fields = [
        (weight.at[dt], held_edges(halos, rows, field, gain[...][None], act, dt * halos, known))
        for dt, field, known in ((2, edges, True), (1, sides, True), (0, edges2, place[4] != 0))
    ]
    for q, part in enumerate(conv_rows(place, halos, rows, fields)):
        value = (before[q] if part is None else before[q] + part).astype(BF16)
        block[in_order(place, q, rows)] = value
        if q == rows - 1:
            near[halos - 1] = value
        elif q == 0 and halos == 2:
            near[0] = value
        else:
            rest[q - (halos - 1)] = value


def up_rows(place, rows, out_rows, pairs, ubias, uw, wide, outs, out_hbm, osems):
    cols = wide.shape[2] // 2
    rest = ubias.shape[-1] - LANES
    chans = uw.shape[1] // 2
    lane = lax.broadcasted_iota(jnp.int32, (cols, LANES), 1)
    stores = []
    for slot_o, o in enumerate(out_rows):
        phase, taken = pairs[o]
        left = jnp.concatenate([jnp.concatenate([r[f] for r in taken], axis=-1) for f in range(2)], axis=0)
        right = uw[phase, (2 - len(taken)) * chans :, :]
        both = jnp.dot(left, right, preferred_element_type=F32)
        for f in range(2):
            part = both[f * cols : (f + 1) * cols]
            g = [part[:, k * LANES : (k + 1) * LANES] for k in range(6)]
            tail = g[4] + jnp.where(lane < rest, moved(g[5], 1), moved(g[5], -1))
            slot = f
            wide[slot, 0, pl.ds(0, cols, stride=2), :] = g[0] + moved(g[2], 1) + ubias[:LANES][None]
            wide[slot, 0, pl.ds(1, cols, stride=2), :] = g[1] + moved(g[3], -1) + ubias[:LANES][None]
            wide[slot, 1, pl.ds(0, cols, stride=2), :] = tail
            wide[slot, 1, pl.ds(1, cols, stride=2), :] = pltpu.roll(tail, LANES - rest, 1)
            outs[f, slot_o, :LANES, :] = wide[slot, 0].T.astype(BF16)
            outs[f, slot_o, LANES:, :] = (wide[slot, 1, :, :rest] + ubias[LANES:][None]).T.astype(BF16)
            copy = pltpu.make_async_copy(
                outs.at[f, slot_o], out_hbm.at[f, in_order(place, o, 2 * rows)], osems.at[f, slot_o]
            )
            copy.start()
            stores.append(copy)
    return stores


def doubled_rows(lefts, tw, tbias, keep):
    cols = lefts[0].shape[0]
    chans = tw.shape[1] // 2
    mixed = jnp.dot(jnp.concatenate(lefts, axis=0), tw[...], preferred_element_type=F32) + tbias[...][None]
    for i in range(len(lefts)):
        for f in range(2):
            keep(i, f, mixed[i * cols : (i + 1) * cols, f * chans : (f + 1) * chans])


def inside(place, halos, h, value):
    return jnp.where(place[1 + h] == 1, value, 0.0) if halos == 2 else value


def row_pairs(halos, rows, at, out_rows):
    lead = halos - 1
    pairs = {}
    for o in out_rows:
        q, phase = divmod(o, 2)
        sources = [s for s in (lead + q - 1 + phase, lead + q + phase) if s >= 0]
        pairs[o] = phase, [[at(s, f) for f in range(2)] for s in sources]
    return pairs


def inner_rows(halos, rows):
    inner = list(range(0 if halos == 1 else 1, 2 * rows - 1))
    return inner, [o for o in range(2 * rows) if o not in inner]


def first_inner(halos, place, own, odd, tbias, ubias, tw, uw, out_hbm, kept, doubled, wide, outs, osems):
    @pl.when(place[4] == 0)
    def _():
        rows = own.shape[0]
        lead = halos - 1
        lefts = []
        for q in range(rows):
            now, before = own[in_order(place, q, rows)], odd[in_order(place, q, rows)]
            none = jnp.zeros_like(now)
            lefts.append(jnp.concatenate([none, jnp.where(place[3] == 0, none, before), now], axis=-1))

        def keep(q, f, value):
            value = value.astype(BF16)
            doubled[f, q] = value
            if q == rows - 1:
                kept[f, halos - 1] = value
            elif q == 0 and halos == 2:
                kept[f, 0] = value

        doubled_rows(lefts, tw, tbias, keep)
        out_rows = inner_rows(halos, rows)[0]
        pairs = row_pairs(halos, rows, lambda s, f: doubled[f, s - lead], out_rows)
        for copy in up_rows(place, rows, out_rows, pairs, ubias, uw, wide, outs, out_hbm, osems):
            copy.wait()


def first_edges(halos, place, edges, odd_edges, kept, tbias, ubias, tw, uw, out_so_far,
                out_hbm, token, doubled, wide, outs, osems):
    del out_so_far
    token[...] = jnp.zeros_like(token)

    @pl.when(place[4] == 0)
    def _():
        rows = out_hbm.shape[1] // 2
        lead = halos - 1
        lefts = []
        for h in range(halos):
            none = jnp.zeros_like(edges[h])
            lefts.append(jnp.concatenate([none, jnp.where(place[3] == 0, none, odd_edges[h]), edges[h]], axis=-1))

        def keep(h, f, value):
            doubled[f, h] = inside(place, halos, h, value).astype(BF16)

        doubled_rows(lefts, tw, tbias, keep)

        def at(s, f):
            if lead <= s < lead + rows:
                return kept[f, 0 if s == lead and halos == 2 else halos - 1]
            return doubled[f, 0 if s < lead else halos - 1]

        out_rows = inner_rows(halos, rows)[1]
        pairs = row_pairs(halos, rows, at, out_rows)
        for copy in up_rows(place, rows, out_rows, pairs, ubias, uw, wide, outs, out_hbm, osems):
            copy.wait()


def up_kernel(halos, place, own, near2, rest2, even_near, even_rest, odd, edges, edges2, even_edges, odd_edges,
              tbias, ubias, tw, uw, token, out_so_far, out_hbm, doubled, wide, outs, osems):
    del token, out_so_far

    @pl.when(place[4] != 0)
    def _():
        rows = own.shape[0]
        lead = halos - 1
        lefts = []
        for s in range(rows + halos):
            if lead <= s < lead + rows:
                q = s - lead
                now, mine = own[in_order(place, q, rows)], odd[in_order(place, q, rows)]
                theirs = parts_row(halos, rows, even_near, even_rest, q)
                first = parts_row(halos, rows, near2, rest2, q)
            else:
                h = 0 if s < lead else halos - 1
                now, mine, theirs, first = edges[h], odd_edges[h], even_edges[h], edges2[h]
            lefts.append(jnp.concatenate([first, jnp.where(place[3] == 0, theirs, mine), now], axis=-1))

        def keep(s, f, value):
            if not lead <= s < lead + rows:
                value = inside(place, halos, 0 if s < lead else halos - 1, value)
            doubled[f, s] = value.astype(BF16)

        doubled_rows(lefts, tw, tbias, keep)
        out_rows = range(2 * rows)
        pairs = row_pairs(halos, rows, lambda s, f: doubled[f, s], out_rows)
        for copy in up_rows(place, rows, out_rows, pairs, ubias, uw, wide, outs, out_hbm, osems):
            copy.wait()


def merge_kernel(place, taps, merged):
    chans = taps.shape[3]

    def tap(dh, dw):
        return taps[in_order(place, dh, 3), dw].astype(F32)

    for phase, sets in enumerate((((0,), (1, 2)), ((0, 1), (2,)))):
        for which, rows in enumerate(sets):
            cols = [sum(tap(dh, dw) for dh in rows) for dw in range(3)]
            groups = (cols[1] + cols[2], cols[0] + cols[1], cols[0], cols[2])
            wide = jnp.concatenate([g[:LANES] for g in groups] + [g[LANES:] for g in groups], axis=0)
            merged[phase, which * chans : (which + 1) * chans, :] = wide.T.astype(BF16)


def in_hbm(array):
    return pltpu.with_memory_space_constraint(array, pltpu.HBM)


def together(*arrays):
    return lax.optimization_barrier(arrays)


def in_chip(array):
    return lax.ppermute(array, "tm", [(i, i ^ 1) for i in range(lax.axis_size("tm"))])


def two_back(array):
    frames = lax.axis_size("tm")
    return lax.ppermute(array, "tm", [(i, (i + 2) % frames) for i in range(frames)])


def beside(near):
    tiles = lax.axis_size("tile")
    if tiles == 2:
        return lax.ppermute(near, "tile", [(0, 1), (1, 0)])
    return jnp.concatenate(
        [
            lax.ppermute(near[1:], "tile", [(j, j + 1) for j in range(tiles - 1)]),
            lax.ppermute(near[:1], "tile", [(j + 1, j) for j in range(tiles - 1)]),
        ]
    )


def local(latent, gain, conv_weight, conv_bias, time_weight, time_bias, up_weight, up_bias):
    tiles = lax.axis_size("tile")
    tile = lax.axis_index("tile")
    frame_at = lax.axis_index("tm")
    halos = 1 if tiles == 2 else 2
    main = latent[0]
    rows, cols, chans = main.shape
    outs_n = up_weight.shape[3]
    flip = tile if halos == 1 else 0 * tile
    place = jnp.stack([flip, tile > 0, tile < tiles - 1, frame_at % 2, frame_at >= 2]).astype(jnp.int32)

    def call(kernel, name, share, ins, outs, scratch, **rest):
        return pl.pallas_call(
            kernel,
            out_shape=tuple(s for s, _ in outs),
            in_specs=[SMEM] + ins,
            out_specs=tuple(s for _, s in outs),
            scratch_shapes=scratch,
            compiler_params=pltpu.CompilerParams(vmem_limit_bytes=20 << 20),
            cost_estimate=pl.CostEstimate(
                flops=int(SHARE * share), bytes_accessed=1000, transcendentals=0
            ),
            name=name,
            **rest,
        )

    field = (rows, cols, chans)
    sides = (halos, cols, chans)

    def conv(kernel, name, share, count):
        step = call(
            functools.partial(kernel, halos), name, share,
            [VMEM] * count,
            [(pltpu.VMEM(field, F32), VMEM)],
            [pltpu.VMEM(field, BF16)],
        )
        return lambda *arrays: step(*arrays)[0]

    taps_t = up_weight.transpose(0, 1, 3, 2)
    merge = call(
        merge_kernel, "merge_taps", MERGE,
        [VMEM],
        [(pltpu.VMEM((2, 2 * chans, 4 * outs_n), BF16), VMEM)],
        [],
    )
    near_rest = [
        (jax.ShapeDtypeStruct(sides, BF16), VMEM),
        (jax.ShapeDtypeStruct((max(rows - halos, 1), cols, chans), BF16), VMEM),
    ]
    if rows == halos:
        other = lambda near, rest, move: near
    else:
        other = lambda near, rest, move: move(rest)

    near, rest = call(functools.partial(split_rows, halos), "split_rows", SPLIT, [VMEM], near_rest, [])(place, main)
    near2 = two_back(near)
    edges = beside(near)
    odd = in_chip(main)
    rest2 = other(near2, rest, two_back)
    acc = conv(conv_first, "conv_own_frame", OWN, 4)(place, main, gain, conv_bias, conv_weight)
    near2, edges, acc = together(near2, edges, acc)
    edges2 = beside(near2)
    even_near = in_chip(near2)
    even_rest = other(even_near, rest2, in_chip)
    odd_edges = in_chip(edges)
    acc = conv(conv_second, "conv_two_back", TWO, 5)(place, near2, rest2, acc, gain, conv_weight)
    edges2, acc = together(edges2, acc)
    even_edges = in_chip(edges2)
    acc = conv(conv_third, "conv_one_back", THREE, 6)(place, even_near, even_rest, odd, acc, gain, conv_weight)
    block, near, rest = call(
        functools.partial(conv_edges, halos), "conv_edge_rows", 1,
        [VMEM] * 7,
        [(jax.ShapeDtypeStruct(field, BF16), VMEM)] + near_rest,
        [pltpu.VMEM((3 * halos, cols, chans), BF16)],
    )(place, edges, edges2, even_edges, odd_edges, acc, gain, conv_weight)

    near2 = two_back(near)
    edges = beside(near)
    odd = in_chip(block)
    taps_t, main = together(taps_t, block)
    (merged,) = merge(place, taps_t)
    tw = time_weight.reshape(3 * chans, 2 * chans)
    out_shape = (jax.ShapeDtypeStruct((2, 2 * rows, outs_n, 2 * cols), BF16), ANY)

    def scratch(count, held):
        return [
            pltpu.VMEM((2, held, cols, chans), BF16),
            pltpu.VMEM((2, 2, 2 * cols, LANES), F32),
            pltpu.VMEM((2, count, outs_n, 2 * cols), BF16),
            pltpu.SemaphoreType.DMA((2, count)),
        ]

    rest, merged = together(rest, merged)
    rest2 = other(near2, rest, two_back)
    common = (time_bias, up_bias, tw, merged)
    inner, outer = (len(o) for o in inner_rows(halos, rows))
    out, kept = call(
        functools.partial(first_inner, halos), "first_chip_inner_rows", FIRST,
        [VMEM] * 6,
        [out_shape, (pltpu.VMEM((2,) + sides, BF16), VMEM)],
        scratch(inner, rows),
    )(place, main, odd, *common)
    near2, kept = together(near2, kept)
    edges2 = beside(near2)
    edges, near2, rest2 = together(edges, near2, rest2)
    even_near = in_chip(near2)
    odd_edges = in_chip(edges)
    even_rest = other(even_near, rest2, in_chip)
    out, token = call(
        functools.partial(first_edges, halos), "first_chip_edge_rows", FIRST,
        [VMEM] * 7 + [ANY],
        [out_shape, (jax.ShapeDtypeStruct((8, LANES), F32), VMEM)],
        scratch(outer, halos),
        input_output_aliases={8: 0},
    )(place, edges, odd_edges, kept, *common, out)
    even_edges = in_chip(edges2)
    (out,) = call(
        functools.partial(up_kernel, halos), "time_and_up", 1,
        [VMEM] * 14 + [ANY] * 2,
        [out_shape],
        scratch(2 * rows, rows + halos),
        input_output_aliases={16: 0},
    )(place, main, near2, rest2, even_near, even_rest, odd, edges, edges2, even_edges, odd_edges,
      *common, token, out)
    return out.transpose(0, 1, 3, 2)


def solution(mesh):
    placed = (P("tm", "tile", None, None), P(), P(), P(), P(), P(), P(), P())
    return jax.shard_map(
        local, mesh=mesh, in_specs=placed, out_specs=P("tm", "tile", None, None), check_vma=False
    )
```

```python
import functools

import jax
import jax.numpy as jnp
from jax import lax
from jax.experimental import pallas as pl
from jax.experimental.pallas import tpu as pltpu
from jax.sharding import PartitionSpec as P

F32 = jnp.float32
BF16 = jnp.bfloat16
VMEM = pl.BlockSpec(memory_space=pltpu.VMEM)
SMEM = pl.BlockSpec(memory_space=pltpu.SMEM)
ANY = pl.BlockSpec(memory_space=pl.ANY)
HBM = pl.BlockSpec(memory_space=pltpu.HBM)
LANES = 128
SHARE = 3000000000
SPLIT = 1
OWN = 0.2
TWO = 0.2
THREE = 1
MERGE = 0.2
FIRST = 0.01


def in_order(place, index, count):
    return jnp.where(place[0] == 1, count - 1 - index, index)


def activate(rows, gain):
    values = rows.astype(F32)
    meansq = jnp.mean(values * values, axis=-1, keepdims=True)
    scaled = values * lax.rsqrt(meansq + 1e-06) * gain
    return (scaled * jax.nn.sigmoid(scaled)).astype(BF16)


def moved(rows, step):
    cols = rows.shape[0]
    index = lax.broadcasted_iota(jnp.int32, rows.shape, 0)
    edge = 0 if step == 1 else cols - 1
    return jnp.where(index == edge, 0.0, pltpu.roll(rows, step % cols, 0))


def conv_rows(place, halos, rows, sources):
    lead = halos - 1
    sums = []
    for q in range(rows):
        lefts, rights = [], []
        for weight, field in sources:
            for dh in range(3):
                s = lead + q + dh - 1
                if s in field:
                    lefts.append(field[s]())
                    tap = in_order(place, dh, 3)
                    rights.append(jnp.concatenate([weight[tap, dw] for dw in range(3)], axis=-1))
        if not lefts:
            sums.append(None)
            continue
        total = jnp.dot(
            jnp.concatenate(lefts, axis=-1), jnp.concatenate(rights, axis=0), preferred_element_type=F32
        )
        chans = total.shape[1] // 3
        sums.append(
            total[:, chans : 2 * chans]
            + moved(total[:, :chans], 1)
            + moved(total[:, 2 * chans :], -1)
        )
    return sums


def hold(act, slot, value):
    act[slot] = value
    return lambda: act[slot]


def parts_row(halos, rows, near, rest, q):
    if halos == 1:
        return near[0] if q == rows - 1 else rest[q]
    if q in (0, rows - 1):
        return near[0 if q == 0 else 1]
    return rest[q - 1]


def held_rows(halos, rows, row, gain, act):
    return {halos - 1 + q: hold(act, q, activate(row(q), gain)) for q in range(rows)}


def held_edges(halos, rows, edges, gain, act, slot, known=True):
    where = (rows,) if halos == 1 else (0, rows + 1)
    return {
        s: hold(act, slot + h, activate(jnp.where(known, edges[h], jnp.zeros_like(edges[h])), gain))
        for h, s in enumerate(where)
    }


def split_rows(halos, place, field, near, rest):
    rows = field.shape[0]
    if halos == 2:
        near[0] = field[0]
    near[halos - 1] = field[in_order(place, rows - 1, rows)]
    for i in range(rows - halos):
        rest[i] = field[in_order(place, halos - 1 + i, rows)]


def conv_first(halos, place, own, gain, bias, weight, acc, act):
    rows = own.shape[0]
    row = lambda q: own[in_order(place, q, rows)]
    field = held_rows(halos, rows, row, gain[...][None], act)
    for q, part in enumerate(conv_rows(place, halos, rows, [(weight.at[2], field)])):
        acc[q] = part + bias[...][None] + row(q).astype(F32)


def conv_second(halos, place, near2, rest2, odd, edges, odd_edges, before, gain, weight, acc, act):
    rows = before.shape[0]

    @pl.when(place[4] == 0)
    def _():
        sides = [one_back(place, odd_edges[h], odd_edges[h]) for h in range(halos)]
        row = lambda q: one_back(place, odd[q], odd[in_order(place, q, rows)])
        field = held_rows(halos, rows, row, gain[...][None], act)
        field.update(held_edges(halos, rows, sides, gain[...][None], act, rows))
        field2 = held_edges(halos, rows, edges, gain[...][None], act, rows + halos)
        for q, part in enumerate(conv_rows(place, halos, rows, [(weight.at[1], field), (weight.at[2], field2)])):
            acc[q] = before[q] + part

    @pl.when(place[4] != 0)
    def _():
        row = lambda q: parts_row(halos, rows, near2, rest2, q)
        field = held_rows(halos, rows, row, gain[...][None], act)
        for q, part in enumerate(conv_rows(place, halos, rows, [(weight.at[0], field)])):
            acc[q] = before[q] + part


def one_back(place, even, odd):
    none = jnp.zeros_like(odd)
    return jnp.where(place[3] != 0, odd, jnp.where(place[4] != 0, even, none))


def conv_third(halos, place, even_near, even_rest, odd, before, gain, weight, acc, act):
    rows = before.shape[0]

    @pl.when(place[4] == 0)
    def _():
        acc[...] = before[...]

    @pl.when(place[4] != 0)
    def _():
        def row(q):
            return one_back(place, parts_row(halos, rows, even_near, even_rest, q), odd[in_order(place, q, rows)])

        field = held_rows(halos, rows, row, gain[...][None], act)
        for q, part in enumerate(conv_rows(place, halos, rows, [(weight.at[1], field)])):
            acc[q] = before[q] + part


def conv_edges(halos, place, edges, edges2, even_edges, odd_edges, before, gain, weight, block, near, rest, act):
    rows = block.shape[0]

    def give(q, value):
        block[in_order(place, q, rows)] = value
        if q == rows - 1:
            near[halos - 1] = value
        elif q == 0 and halos == 2:
            near[0] = value
        else:
            rest[q - (halos - 1)] = value

    @pl.when(place[4] == 0)
    def _():
        for q in range(rows):
            give(q, before[q].astype(BF16))

    @pl.when(place[4] != 0)
    def _():
        sides = [one_back(place, even_edges[h], odd_edges[h]) for h in range(halos)]
        fields = [
            (weight.at[dt], held_edges(halos, rows, field, gain[...][None], act, dt * halos))
            for dt, field in ((2, edges), (1, sides), (0, edges2))
        ]
        for q, part in enumerate(conv_rows(place, halos, rows, fields)):
            give(q, (before[q] if part is None else before[q] + part).astype(BF16))


def up_rows(place, rows, out_rows, pairs, ubias, uw, wide, outs, out_hbm, osems):
    cols = wide.shape[2] // 2
    rest = ubias.shape[-1] - LANES
    chans = uw.shape[1] // 2
    lane = lax.broadcasted_iota(jnp.int32, (cols, LANES), 1)
    stores = []
    for slot_o, o in enumerate(out_rows):
        phase, taken = pairs[o]
        left = jnp.concatenate([jnp.concatenate([r[f] for r in taken], axis=-1) for f in range(2)], axis=0)
        right = uw[phase, (2 - len(taken)) * chans :, :]
        both = jnp.dot(left, right, preferred_element_type=F32)
        for f in range(2):
            part = both[f * cols : (f + 1) * cols]
            g = [part[:, k * LANES : (k + 1) * LANES] for k in range(6)]
            tail = g[4] + jnp.where(lane < rest, moved(g[5], 1), moved(g[5], -1))
            slot = f
            wide[slot, 0, pl.ds(0, cols, stride=2), :] = g[0] + moved(g[2], 1) + ubias[:LANES][None]
            wide[slot, 0, pl.ds(1, cols, stride=2), :] = g[1] + moved(g[3], -1) + ubias[:LANES][None]
            wide[slot, 1, pl.ds(0, cols, stride=2), :] = tail
            wide[slot, 1, pl.ds(1, cols, stride=2), :] = pltpu.roll(tail, LANES - rest, 1)
            outs[f, slot_o, :LANES, :] = wide[slot, 0].T.astype(BF16)
            outs[f, slot_o, LANES:, :] = (wide[slot, 1, :, :rest] + ubias[LANES:][None]).T.astype(BF16)
            copy = pltpu.make_async_copy(
                outs.at[f, slot_o], out_hbm.at[f, in_order(place, o, 2 * rows)], osems.at[f, slot_o]
            )
            copy.start()
            stores.append(copy)
    return stores


def doubled_rows(lefts, tw, tbias, keep):
    cols = lefts[0].shape[0]
    chans = tw.shape[1] // 2
    mixed = jnp.dot(jnp.concatenate(lefts, axis=0), tw[...], preferred_element_type=F32) + tbias[...][None]
    for i in range(len(lefts)):
        for f in range(2):
            keep(i, f, mixed[i * cols : (i + 1) * cols, f * chans : (f + 1) * chans])


def inside(place, halos, h, value):
    return jnp.where(place[1 + h] == 1, value, 0.0) if halos == 2 else value


def row_pairs(halos, rows, at, out_rows):
    lead = halos - 1
    pairs = {}
    for o in out_rows:
        q, phase = divmod(o, 2)
        sources = [s for s in (lead + q - 1 + phase, lead + q + phase) if s >= 0]
        pairs[o] = phase, [[at(s, f) for f in range(2)] for s in sources]
    return pairs


def inner_rows(halos, rows):
    inner = list(range(0 if halos == 1 else 1, 2 * rows - 1))
    return inner, [o for o in range(2 * rows) if o not in inner]


def first_rows(halos, rows):
    inner, outer = inner_rows(halos, rows)
    half = (len(inner) + 1) // 2
    return inner[:half], inner[half:] + outer


def first_inner(halos, place, own, odd, tbias, ubias, tw, uw, out_hbm, kept, wide, outs, osems):
    @pl.when(place[4] == 0)
    def _():
        rows = own.shape[0]
        lead = halos - 1
        lefts = []
        for q in range(rows):
            now, before = own[in_order(place, q, rows)], odd[in_order(place, q, rows)]
            none = jnp.zeros_like(now)
            lefts.append(jnp.concatenate([none, jnp.where(place[3] == 0, none, before), now], axis=-1))

        def keep(q, f, value):
            kept[f, q] = value.astype(BF16)

        doubled_rows(lefts, tw, tbias, keep)
        out_rows = first_rows(halos, rows)[0]
        pairs = row_pairs(halos, rows, lambda s, f: kept[f, s - lead], out_rows)
        for copy in up_rows(place, rows, out_rows, pairs, ubias, uw, wide, outs, out_hbm, osems):
            copy.wait()


def first_edges(halos, place, edges, odd_edges, kept, tbias, ubias, tw, uw, out_so_far,
                out_hbm, token, doubled, wide, outs, osems):
    del out_so_far
    token[...] = jnp.zeros_like(token)

    @pl.when(place[4] == 0)
    def _():
        rows = out_hbm.shape[1] // 2
        lead = halos - 1
        lefts = []
        for h in range(halos):
            none = jnp.zeros_like(edges[h])
            lefts.append(jnp.concatenate([none, jnp.where(place[3] == 0, none, odd_edges[h]), edges[h]], axis=-1))

        def keep(h, f, value):
            doubled[f, h] = inside(place, halos, h, value).astype(BF16)

        doubled_rows(lefts, tw, tbias, keep)

        def at(s, f):
            if lead <= s < lead + rows:
                return kept[f, s - lead]
            return doubled[f, 0 if s < lead else halos - 1]

        out_rows = first_rows(halos, rows)[1]
        pairs = row_pairs(halos, rows, at, out_rows)
        for copy in up_rows(place, rows, out_rows, pairs, ubias, uw, wide, outs, out_hbm, osems):
            copy.wait()


def up_kernel(halos, place, own, near2, rest2, even_near, even_rest, odd, edges, edges2, even_edges, odd_edges,
              tbias, ubias, tw, uw, token, out_so_far, out_hbm, doubled, wide, outs, osems):
    del token, out_so_far

    @pl.when(place[4] != 0)
    def _():
        rows = own.shape[0]
        lead = halos - 1
        lefts = []
        for s in range(rows + halos):
            if lead <= s < lead + rows:
                q = s - lead
                now, mine = own[in_order(place, q, rows)], odd[in_order(place, q, rows)]
                theirs = parts_row(halos, rows, even_near, even_rest, q)
                first = parts_row(halos, rows, near2, rest2, q)
            else:
                h = 0 if s < lead else halos - 1
                now, mine, theirs, first = edges[h], odd_edges[h], even_edges[h], edges2[h]
            lefts.append(jnp.concatenate([first, jnp.where(place[3] == 0, theirs, mine), now], axis=-1))

        def keep(s, f, value):
            if not lead <= s < lead + rows:
                value = inside(place, halos, 0 if s < lead else halos - 1, value)
            doubled[f, s] = value.astype(BF16)

        doubled_rows(lefts, tw, tbias, keep)
        out_rows = range(2 * rows)
        pairs = row_pairs(halos, rows, lambda s, f: doubled[f, s], out_rows)
        for copy in up_rows(place, rows, out_rows, pairs, ubias, uw, wide, outs, out_hbm, osems):
            copy.wait()


def merge_kernel(place, taps, merged):
    chans = taps.shape[3]

    def tap(dh, dw):
        return taps[in_order(place, dh, 3), dw].astype(F32)

    for phase, sets in enumerate((((0,), (1, 2)), ((0, 1), (2,)))):
        for which, rows in enumerate(sets):
            cols = [sum(tap(dh, dw) for dh in rows) for dw in range(3)]
            groups = (cols[1] + cols[2], cols[0] + cols[1], cols[0], cols[2])
            wide = jnp.concatenate([g[:LANES] for g in groups] + [g[LANES:] for g in groups], axis=0)
            merged[phase, which * chans : (which + 1) * chans, :] = wide.T.astype(BF16)


def in_hbm(array):
    return pltpu.with_memory_space_constraint(array, pltpu.HBM)


def together(*arrays):
    return lax.optimization_barrier(arrays)


def in_chip(array):
    return lax.ppermute(array, "tm", [(i, i ^ 1) for i in range(lax.axis_size("tm"))])


def two_back(array):
    frames = lax.axis_size("tm")
    return lax.ppermute(array, "tm", [(i, (i + 2) % frames) for i in range(frames)])


def beside(near):
    tiles = lax.axis_size("tile")
    if tiles == 2:
        return lax.ppermute(near, "tile", [(0, 1), (1, 0)])
    return jnp.concatenate(
        [
            lax.ppermute(near[1:], "tile", [(j, j + 1) for j in range(tiles - 1)]),
            lax.ppermute(near[:1], "tile", [(j + 1, j) for j in range(tiles - 1)]),
        ]
    )


def local(latent, gain, conv_weight, conv_bias, time_weight, time_bias, up_weight, up_bias):
    tiles = lax.axis_size("tile")
    tile = lax.axis_index("tile")
    frame_at = lax.axis_index("tm")
    halos = 1 if tiles == 2 else 2
    main = latent[0]
    rows, cols, chans = main.shape
    outs_n = up_weight.shape[3]
    flip = tile if halos == 1 else 0 * tile
    place = jnp.stack([flip, tile > 0, tile < tiles - 1, frame_at % 2, frame_at >= 2]).astype(jnp.int32)

    def call(kernel, name, share, ins, outs, scratch, **rest):
        return pl.pallas_call(
            kernel,
            out_shape=tuple(s for s, _ in outs),
            in_specs=[SMEM] + ins,
            out_specs=tuple(s for _, s in outs),
            scratch_shapes=scratch,
            compiler_params=pltpu.CompilerParams(vmem_limit_bytes=20 << 20),
            cost_estimate=pl.CostEstimate(
                flops=int(SHARE * share), bytes_accessed=1000, transcendentals=0
            ),
            name=name,
            **rest,
        )

    field = (rows, cols, chans)
    sides = (halos, cols, chans)

    def conv(kernel, name, share, count, more=0):
        step = call(
            functools.partial(kernel, halos), name, share,
            [VMEM] * count,
            [(pltpu.VMEM(field, F32), VMEM)],
            [pltpu.VMEM((rows + more, cols, chans), BF16)],
        )
        return lambda *arrays: step(*arrays)[0]

    taps_t = up_weight.transpose(0, 1, 3, 2)
    merge = call(
        merge_kernel, "merge_taps", MERGE,
        [VMEM],
        [(pltpu.VMEM((2, 2 * chans, 4 * outs_n), BF16), VMEM)],
        [],
    )
    near_rest = [
        (jax.ShapeDtypeStruct(sides, BF16), VMEM),
        (jax.ShapeDtypeStruct((max(rows - halos, 1), cols, chans), BF16), VMEM),
    ]
    if rows == halos:
        other = lambda near, rest, move: near
    else:
        other = lambda near, rest, move: move(rest)

    near, rest = call(functools.partial(split_rows, halos), "split_rows", SPLIT, [VMEM], near_rest, [])(place, in_hbm(main))
    near2 = two_back(near)
    edges = beside(near)
    odd = in_chip(main)
    rest2 = other(near2, rest, two_back)
    acc = conv(conv_first, "conv_own_frame", OWN, 4)(place, main, gain, conv_bias, conv_weight)
    near2, edges, acc = together(near2, edges, acc)
    edges2 = beside(near2)
    odd_edges = in_chip(edges)
    even_near = in_chip(near2)
    even_rest = other(even_near, rest2, in_chip)
    acc = conv(conv_second, "conv_two_back", TWO, 8, 2 * halos)(
        place, near2, rest2, odd, edges, odd_edges, acc, gain, conv_weight
    )
    edges2, acc = together(edges2, acc)
    even_edges = in_chip(edges2)
    acc = conv(conv_third, "conv_one_back", THREE, 6)(place, even_near, even_rest, odd, acc, gain, conv_weight)
    block, near, rest = call(
        functools.partial(conv_edges, halos), "conv_edge_rows", 1,
        [VMEM] * 7,
        [(jax.ShapeDtypeStruct(field, BF16), VMEM)] + near_rest,
        [pltpu.VMEM((3 * halos, cols, chans), BF16)],
    )(place, edges, edges2, even_edges, odd_edges, acc, gain, conv_weight)

    near2 = two_back(near)
    edges = beside(near)
    odd = in_chip(block)
    taps_t, main = together(taps_t, block)
    (merged,) = merge(place, taps_t)
    tw = time_weight.reshape(3 * chans, 2 * chans)
    out_shape = (jax.ShapeDtypeStruct((2, 2 * rows, outs_n, 2 * cols), BF16), ANY)

    def scratch(count, held):
        return [
            pltpu.VMEM((2, held, cols, chans), BF16),
            pltpu.VMEM((2, 2, 2 * cols, LANES), F32),
            pltpu.VMEM((2, count, outs_n, 2 * cols), BF16),
            pltpu.SemaphoreType.DMA((2, count)),
        ]

    rest, merged = together(rest, merged)
    rest2 = other(near2, rest, two_back)
    common = (time_bias, up_bias, tw, merged)
    one, two = (len(o) for o in first_rows(halos, rows))
    out, kept = call(
        functools.partial(first_inner, halos), "first_chip_inner_rows", FIRST,
        [VMEM] * 6,
        [out_shape, (pltpu.VMEM((2,) + field, BF16), VMEM)],
        scratch(one, rows)[1:],
    )(place, main, odd, *common)
    near2, kept = together(near2, kept)
    edges2 = beside(near2)
    edges, near2 = together(edges, near2)
    odd_edges = in_chip(edges)
    near2, rest2, kept = together(near2, rest2, kept)
    even_near = in_chip(near2)
    even_rest = other(even_near, rest2, in_chip)
    out, token = call(
        functools.partial(first_edges, halos), "first_chip_edge_rows", FIRST,
        [VMEM] * 7 + [ANY],
        [out_shape, (jax.ShapeDtypeStruct((8, LANES), F32), VMEM)],
        scratch(two, halos),
        input_output_aliases={8: 0},
    )(place, edges, odd_edges, kept, *common, out)
    edges2, token = together(edges2, token)
    even_edges = in_chip(edges2)
    (out,) = call(
        functools.partial(up_kernel, halos), "time_and_up", 1,
        [VMEM] * 14 + [ANY] * 2,
        [out_shape],
        scratch(2 * rows, rows + halos),
        input_output_aliases={16: 0},
    )(place, main, near2, rest2, even_near, even_rest, odd, edges, edges2, even_edges, odd_edges,
      *common, token, out)
    return out.transpose(0, 1, 3, 2)


def solution(mesh):
    placed = (P("tm", "tile", None, None), P(), P(), P(), P(), P(), P(), P())
    return jax.shard_map(
        local, mesh=mesh, in_specs=placed, out_specs=P("tm", "tile", None, None), check_vma=False
    )
```

```python
import functools

import jax
import jax.numpy as jnp
from jax import lax
from jax.experimental import pallas as pl
from jax.experimental.pallas import tpu as pltpu
from jax.sharding import PartitionSpec as P

F32 = jnp.float32
BF16 = jnp.bfloat16
VMEM = pl.BlockSpec(memory_space=pltpu.VMEM)
SMEM = pl.BlockSpec(memory_space=pltpu.SMEM)
ANY = pl.BlockSpec(memory_space=pl.ANY)
HBM = pl.BlockSpec(memory_space=pltpu.HBM)
LANES = 128
SHARE = 3000000000
SPLIT = 1
OWN = 0.2
TWO = 0.2
THREE = 1
MERGE = 0.2
FIRST = 0.01


def in_order(place, index, count):
    return jnp.where(place[0] == 1, count - 1 - index, index)


def activate(rows, gain):
    values = rows.astype(F32)
    meansq = jnp.mean(values * values, axis=-1, keepdims=True)
    scaled = values * lax.rsqrt(meansq + 1e-06) * gain
    return (scaled * jax.nn.sigmoid(scaled)).astype(BF16)


def moved(rows, step):
    cols = rows.shape[0]
    index = lax.broadcasted_iota(jnp.int32, rows.shape, 0)
    edge = 0 if step == 1 else cols - 1
    return jnp.where(index == edge, 0.0, pltpu.roll(rows, step % cols, 0))


def conv_rows(place, halos, rows, sources):
    lead = halos - 1
    sums = []
    for q in range(rows):
        lefts, rights = [], []
        for weight, field in sources:
            for dh in range(3):
                s = lead + q + dh - 1
                if s in field:
                    lefts.append(field[s]())
                    tap = in_order(place, dh, 3)
                    rights.append(jnp.concatenate([weight[tap, dw] for dw in range(3)], axis=-1))
        if not lefts:
            sums.append(None)
            continue
        total = jnp.dot(
            jnp.concatenate(lefts, axis=-1), jnp.concatenate(rights, axis=0), preferred_element_type=F32
        )
        chans = total.shape[1] // 3
        sums.append(
            total[:, chans : 2 * chans]
            + moved(total[:, :chans], 1)
            + moved(total[:, 2 * chans :], -1)
        )
    return sums


def hold(act, slot, value):
    act[slot] = value
    return lambda: act[slot]


def parts_row(halos, rows, near, rest, q):
    if halos == 1:
        return near[0] if q == rows - 1 else rest[q]
    if q in (0, rows - 1):
        return near[0 if q == 0 else 1]
    return rest[q - 1]


def held_rows(halos, rows, row, gain, act):
    return {halos - 1 + q: hold(act, q, activate(row(q), gain)) for q in range(rows)}


def held_edges(halos, rows, edges, gain, act, slot, known=True):
    where = (rows,) if halos == 1 else (0, rows + 1)
    return {
        s: hold(act, slot + h, activate(jnp.where(known, edges[h], jnp.zeros_like(edges[h])), gain))
        for h, s in enumerate(where)
    }


def split_rows(halos, place, field, near, rest):
    rows = field.shape[0]
    if halos == 2:
        near[0] = field[0]
    near[halos - 1] = field[in_order(place, rows - 1, rows)]
    for i in range(rows - halos):
        rest[i] = field[in_order(place, halos - 1 + i, rows)]


def conv_first(halos, place, own, gain, bias, weight, acc, act):
    rows = own.shape[0]
    row = lambda q: own[in_order(place, q, rows)]
    field = held_rows(halos, rows, row, gain[...][None], act)
    for q, part in enumerate(conv_rows(place, halos, rows, [(weight.at[2], field)])):
        acc[q] = part + bias[...][None] + row(q).astype(F32)


def conv_second(halos, place, near2, rest2, odd, edges, odd_edges, before, gain, weight, acc, act):
    rows = before.shape[0]

    @pl.when(place[4] == 0)
    def _():
        sides = [one_back(place, odd_edges[h], odd_edges[h]) for h in range(halos)]
        row = lambda q: one_back(place, odd[q], odd[in_order(place, q, rows)])
        field = held_rows(halos, rows, row, gain[...][None], act)
        field.update(held_edges(halos, rows, sides, gain[...][None], act, rows))
        field2 = held_edges(halos, rows, edges, gain[...][None], act, rows + halos)
        for q, part in enumerate(conv_rows(place, halos, rows, [(weight.at[1], field), (weight.at[2], field2)])):
            acc[q] = before[q] + part

    @pl.when(place[4] != 0)
    def _():
        row = lambda q: parts_row(halos, rows, near2, rest2, q)
        field = held_rows(halos, rows, row, gain[...][None], act)
        for q, part in enumerate(conv_rows(place, halos, rows, [(weight.at[0], field)])):
            acc[q] = before[q] + part


def one_back(place, even, odd):
    none = jnp.zeros_like(odd)
    return jnp.where(place[3] != 0, odd, jnp.where(place[4] != 0, even, none))


def conv_third(halos, place, even_near, even_rest, odd, before, gain, weight, acc, act):
    rows = before.shape[0]

    @pl.when(place[4] == 0)
    def _():
        acc[...] = before[...]

    @pl.when(place[4] != 0)
    def _():
        def row(q):
            return one_back(place, parts_row(halos, rows, even_near, even_rest, q), odd[in_order(place, q, rows)])

        field = held_rows(halos, rows, row, gain[...][None], act)
        for q, part in enumerate(conv_rows(place, halos, rows, [(weight.at[1], field)])):
            acc[q] = before[q] + part


def conv_edges(halos, place, edges, edges2, even_edges, odd_edges, before, gain, weight, block, near, rest, act):
    rows = block.shape[0]

    def give(q, value):
        block[in_order(place, q, rows)] = value
        if q == rows - 1:
            near[halos - 1] = value
        elif q == 0 and halos == 2:
            near[0] = value
        else:
            rest[q - (halos - 1)] = value

    @pl.when(place[4] == 0)
    def _():
        for q in range(rows):
            give(q, before[q].astype(BF16))

    @pl.when(place[4] != 0)
    def _():
        sides = [one_back(place, even_edges[h], odd_edges[h]) for h in range(halos)]
        fields = [
            (weight.at[dt], held_edges(halos, rows, field, gain[...][None], act, dt * halos))
            for dt, field in ((2, edges), (1, sides), (0, edges2))
        ]
        for q, part in enumerate(conv_rows(place, halos, rows, fields)):
            give(q, (before[q] if part is None else before[q] + part).astype(BF16))


def up_rows(place, rows, out_rows, pairs, ubias, uw, wide, outs, out_hbm, osems):
    cols = wide.shape[2] // 2
    rest = ubias.shape[-1] - LANES
    chans = uw.shape[1] // 2
    lane = lax.broadcasted_iota(jnp.int32, (cols, LANES), 1)
    stores = []
    for slot_o, o in enumerate(out_rows):
        phase, taken = pairs[o]
        left = jnp.concatenate([jnp.concatenate([r[f] for r in taken], axis=-1) for f in range(2)], axis=0)
        right = uw[phase, (2 - len(taken)) * chans :, :]
        both = jnp.dot(left, right, preferred_element_type=F32)
        for f in range(2):
            part = both[f * cols : (f + 1) * cols]
            g = [part[:, k * LANES : (k + 1) * LANES] for k in range(6)]
            tail = g[4] + jnp.where(lane < rest, moved(g[5], 1), moved(g[5], -1))
            slot = f
            wide[slot, 0, pl.ds(0, cols, stride=2), :] = g[0] + moved(g[2], 1) + ubias[:LANES][None]
            wide[slot, 0, pl.ds(1, cols, stride=2), :] = g[1] + moved(g[3], -1) + ubias[:LANES][None]
            wide[slot, 1, pl.ds(0, cols, stride=2), :] = tail
            wide[slot, 1, pl.ds(1, cols, stride=2), :] = pltpu.roll(tail, LANES - rest, 1)
            outs[f, slot_o, :LANES, :] = wide[slot, 0].T.astype(BF16)
            outs[f, slot_o, LANES:, :] = (wide[slot, 1, :, :rest] + ubias[LANES:][None]).T.astype(BF16)
            copy = pltpu.make_async_copy(
                outs.at[f, slot_o], out_hbm.at[f, in_order(place, o, 2 * rows)], osems.at[f, slot_o]
            )
            copy.start()
            stores.append(copy)
    return stores


def doubled_rows(lefts, tw, tbias, keep):
    cols = lefts[0].shape[0]
    chans = tw.shape[1] // 2
    mixed = jnp.dot(jnp.concatenate(lefts, axis=0), tw[...], preferred_element_type=F32) + tbias[...][None]
    for i in range(len(lefts)):
        for f in range(2):
            keep(i, f, mixed[i * cols : (i + 1) * cols, f * chans : (f + 1) * chans])


def inside(place, halos, h, value):
    return jnp.where(place[1 + h] == 1, value, 0.0) if halos == 2 else value


def row_pairs(halos, rows, at, out_rows):
    lead = halos - 1
    pairs = {}
    for o in out_rows:
        q, phase = divmod(o, 2)
        sources = [s for s in (lead + q - 1 + phase, lead + q + phase) if s >= 0]
        pairs[o] = phase, [[at(s, f) for f in range(2)] for s in sources]
    return pairs


def inner_rows(halos, rows):
    inner = list(range(0 if halos == 1 else 1, 2 * rows - 1))
    return inner, [o for o in range(2 * rows) if o not in inner]


def first_rows(halos, rows):
    inner, outer = inner_rows(halos, rows)
    half = (len(inner) + 1) // 2
    return inner[:half], inner[half:] + outer


def merge_and_first(halos, place, taps, own, odd, tbias, ubias, tw, uw, out_hbm, kept, wide, outs, osems):
    merge_taps(place, taps, uw)

    @pl.when(place[4] == 0)
    def _():
        rows = own.shape[0]
        lead = halos - 1
        lefts = []
        for q in range(rows):
            now, before = own[in_order(place, q, rows)], odd[in_order(place, q, rows)]
            none = jnp.zeros_like(now)
            lefts.append(jnp.concatenate([none, jnp.where(place[3] == 0, none, before), now], axis=-1))

        def keep(q, f, value):
            kept[f, q] = value.astype(BF16)

        doubled_rows(lefts, tw, tbias, keep)
        out_rows = first_rows(halos, rows)[0]
        pairs = row_pairs(halos, rows, lambda s, f: kept[f, s - lead], out_rows)
        for copy in up_rows(place, rows, out_rows, pairs, ubias, uw, wide, outs, out_hbm, osems):
            copy.wait()


def first_edges(halos, place, edges, odd_edges, kept, tbias, ubias, tw, uw, out_so_far,
                out_hbm, token, doubled, wide, outs, osems):
    del out_so_far
    token[...] = jnp.zeros_like(token)

    @pl.when(place[4] == 0)
    def _():
        rows = out_hbm.shape[1] // 2
        lead = halos - 1
        lefts = []
        for h in range(halos):
            none = jnp.zeros_like(edges[h])
            lefts.append(jnp.concatenate([none, jnp.where(place[3] == 0, none, odd_edges[h]), edges[h]], axis=-1))

        def keep(h, f, value):
            doubled[f, h] = inside(place, halos, h, value).astype(BF16)

        doubled_rows(lefts, tw, tbias, keep)

        def at(s, f):
            if lead <= s < lead + rows:
                return kept[f, s - lead]
            return doubled[f, 0 if s < lead else halos - 1]

        out_rows = first_rows(halos, rows)[1]
        pairs = row_pairs(halos, rows, at, out_rows)
        for copy in up_rows(place, rows, out_rows, pairs, ubias, uw, wide, outs, out_hbm, osems):
            copy.wait()


def up_kernel(halos, place, own, near2, rest2, even_near, even_rest, odd, edges, edges2, even_edges, odd_edges,
              tbias, ubias, tw, uw, token, out_so_far, out_hbm, doubled, wide, outs, osems):
    del token, out_so_far

    @pl.when(place[4] != 0)
    def _():
        rows = own.shape[0]
        lead = halos - 1
        lefts = []
        for s in range(rows + halos):
            if lead <= s < lead + rows:
                q = s - lead
                now, mine = own[in_order(place, q, rows)], odd[in_order(place, q, rows)]
                theirs = parts_row(halos, rows, even_near, even_rest, q)
                first = parts_row(halos, rows, near2, rest2, q)
            else:
                h = 0 if s < lead else halos - 1
                now, mine, theirs, first = edges[h], odd_edges[h], even_edges[h], edges2[h]
            lefts.append(jnp.concatenate([first, jnp.where(place[3] == 0, theirs, mine), now], axis=-1))

        def keep(s, f, value):
            if not lead <= s < lead + rows:
                value = inside(place, halos, 0 if s < lead else halos - 1, value)
            doubled[f, s] = value.astype(BF16)

        doubled_rows(lefts, tw, tbias, keep)
        out_rows = range(2 * rows)
        pairs = row_pairs(halos, rows, lambda s, f: doubled[f, s], out_rows)
        for copy in up_rows(place, rows, out_rows, pairs, ubias, uw, wide, outs, out_hbm, osems):
            copy.wait()


def merge_taps(place, taps, merged):
    chans = taps.shape[3]

    def tap(dh, dw):
        return taps[in_order(place, dh, 3), dw].astype(F32)

    for phase, sets in enumerate((((0,), (1, 2)), ((0, 1), (2,)))):
        for which, rows in enumerate(sets):
            cols = [sum(tap(dh, dw) for dh in rows) for dw in range(3)]
            groups = (cols[1] + cols[2], cols[0] + cols[1], cols[0], cols[2])
            wide = jnp.concatenate([g[:LANES] for g in groups] + [g[LANES:] for g in groups], axis=0)
            merged[phase, which * chans : (which + 1) * chans, :] = wide.T.astype(BF16)


def in_hbm(array):
    return pltpu.with_memory_space_constraint(array, pltpu.HBM)


def together(*arrays):
    return lax.optimization_barrier(arrays)


def in_chip(array):
    return lax.ppermute(array, "tm", [(i, i ^ 1) for i in range(lax.axis_size("tm"))])


def two_back(array):
    frames = lax.axis_size("tm")
    return lax.ppermute(array, "tm", [(i, (i + 2) % frames) for i in range(frames)])


def beside(near):
    tiles = lax.axis_size("tile")
    if tiles == 2:
        return lax.ppermute(near, "tile", [(0, 1), (1, 0)])
    return jnp.concatenate(
        [
            lax.ppermute(near[1:], "tile", [(j, j + 1) for j in range(tiles - 1)]),
            lax.ppermute(near[:1], "tile", [(j + 1, j) for j in range(tiles - 1)]),
        ]
    )


def local(latent, gain, conv_weight, conv_bias, time_weight, time_bias, up_weight, up_bias):
    tiles = lax.axis_size("tile")
    tile = lax.axis_index("tile")
    frame_at = lax.axis_index("tm")
    halos = 1 if tiles == 2 else 2
    main = latent[0]
    rows, cols, chans = main.shape
    outs_n = up_weight.shape[3]
    flip = tile if halos == 1 else 0 * tile
    place = jnp.stack([flip, tile > 0, tile < tiles - 1, frame_at % 2, frame_at >= 2]).astype(jnp.int32)

    def call(kernel, name, share, ins, outs, scratch, **rest):
        return pl.pallas_call(
            kernel,
            out_shape=tuple(s for s, _ in outs),
            in_specs=[SMEM] + ins,
            out_specs=tuple(s for _, s in outs),
            scratch_shapes=scratch,
            compiler_params=pltpu.CompilerParams(vmem_limit_bytes=20 << 20),
            cost_estimate=pl.CostEstimate(
                flops=int(SHARE * share), bytes_accessed=1000, transcendentals=0
            ),
            name=name,
            **rest,
        )

    field = (rows, cols, chans)
    sides = (halos, cols, chans)

    def conv(kernel, name, share, count, more=0):
        step = call(
            functools.partial(kernel, halos), name, share,
            [VMEM] * count,
            [(pltpu.VMEM(field, F32), VMEM)],
            [pltpu.VMEM((rows + more, cols, chans), BF16)],
        )
        return lambda *arrays: step(*arrays)[0]

    taps_t = up_weight.transpose(0, 1, 3, 2)
    near_rest = [
        (jax.ShapeDtypeStruct(sides, BF16), VMEM),
        (jax.ShapeDtypeStruct((max(rows - halos, 1), cols, chans), BF16), VMEM),
    ]
    if rows == halos:
        other = lambda near, rest, move: near
    else:
        other = lambda near, rest, move: move(rest)

    near, rest = call(functools.partial(split_rows, halos), "split_rows", SPLIT, [VMEM], near_rest, [])(place, in_hbm(main))
    near2 = two_back(near)
    edges = beside(near)
    odd = in_chip(main)
    rest2 = other(near2, rest, two_back)
    acc = conv(conv_first, "conv_own_frame", OWN, 4)(place, main, gain, conv_bias, conv_weight)
    near2, edges, acc = together(near2, edges, acc)
    edges2 = beside(near2)
    odd_edges = in_chip(edges)
    even_near = in_chip(near2)
    even_rest = other(even_near, rest2, in_chip)
    acc = conv(conv_second, "conv_two_back", TWO, 8, 2 * halos)(
        place, near2, rest2, odd, edges, odd_edges, acc, gain, conv_weight
    )
    edges2, acc = together(edges2, acc)
    even_edges = in_chip(edges2)
    acc = conv(conv_third, "conv_one_back", THREE, 6)(place, even_near, even_rest, odd, acc, gain, conv_weight)
    block, near, rest = call(
        functools.partial(conv_edges, halos), "conv_edge_rows", 1,
        [VMEM] * 7,
        [(jax.ShapeDtypeStruct(field, BF16), VMEM)] + near_rest,
        [pltpu.VMEM((3 * halos, cols, chans), BF16)],
    )(place, edges, edges2, even_edges, odd_edges, acc, gain, conv_weight)

    near2 = two_back(near)
    edges = beside(near)
    odd = in_chip(block)
    taps_t, main = together(taps_t, block)
    tw = time_weight.reshape(3 * chans, 2 * chans)
    out_shape = (jax.ShapeDtypeStruct((2, 2 * rows, outs_n, 2 * cols), BF16), ANY)

    def scratch(count, held):
        return [
            pltpu.VMEM((2, held, cols, chans), BF16),
            pltpu.VMEM((2, 2, 2 * cols, LANES), F32),
            pltpu.VMEM((2, count, outs_n, 2 * cols), BF16),
            pltpu.SemaphoreType.DMA((2, count)),
        ]

    rest2 = other(near2, rest, two_back)
    one, two = (len(o) for o in first_rows(halos, rows))
    merged, out, kept = call(
        functools.partial(merge_and_first, halos), "merge_taps_and_first_chip_rows", MERGE,
        [VMEM] * 6,
        [
            (pltpu.VMEM((2, 2 * chans, 4 * outs_n), BF16), VMEM),
            out_shape,
            (pltpu.VMEM((2,) + field, BF16), VMEM),
        ],
        scratch(one, rows)[1:],
    )(place, taps_t, main, odd, time_bias, up_bias, tw)
    common = (time_bias, up_bias, tw, merged)
    near2, kept = together(near2, kept)
    edges2 = beside(near2)
    edges, near2 = together(edges, near2)
    odd_edges = in_chip(edges)
    near2, rest2, kept = together(near2, rest2, kept)
    even_near = in_chip(near2)
    even_rest = other(even_near, rest2, in_chip)
    out, token = call(
        functools.partial(first_edges, halos), "first_chip_edge_rows", FIRST,
        [VMEM] * 7 + [ANY],
        [out_shape, (jax.ShapeDtypeStruct((8, LANES), F32), VMEM)],
        scratch(two, halos),
        input_output_aliases={8: 0},
    )(place, edges, odd_edges, kept, *common, out)
    even_edges = in_chip(edges2)
    (out,) = call(
        functools.partial(up_kernel, halos), "time_and_up", 1,
        [VMEM] * 14 + [ANY] * 2,
        [out_shape],
        scratch(2 * rows, rows + halos),
        input_output_aliases={16: 0},
    )(place, main, near2, rest2, even_near, even_rest, odd, edges, edges2, even_edges, odd_edges,
      *common, token, out)
    return out.transpose(0, 1, 3, 2)


def solution(mesh):
    placed = (P("tm", "tile", None, None), P(), P(), P(), P(), P(), P(), P())
    return jax.shard_map(
        local, mesh=mesh, in_specs=placed, out_specs=P("tm", "tile", None, None), check_vma=False
    )
```

```python
import functools

import jax
import jax.numpy as jnp
from jax import lax
from jax.experimental import pallas as pl
from jax.experimental.pallas import tpu as pltpu
from jax.sharding import PartitionSpec as P

F32 = jnp.float32
BF16 = jnp.bfloat16
VMEM = pl.BlockSpec(memory_space=pltpu.VMEM)
SMEM = pl.BlockSpec(memory_space=pltpu.SMEM)
ANY = pl.BlockSpec(memory_space=pl.ANY)
HBM = pl.BlockSpec(memory_space=pltpu.HBM)
LANES = 128
SHARE = 3000000000
SPLIT = 1
OWN = 0.2
TWO = 0.2
THREE = 1
MERGE = 0.2
FIRST = 0.01


def in_order(place, index, count):
    return jnp.where(place[0] == 1, count - 1 - index, index)


def activate(rows, gain):
    values = rows.astype(F32)
    meansq = jnp.mean(values * values, axis=-1, keepdims=True)
    scaled = values * lax.rsqrt(meansq + 1e-06) * gain
    return (scaled * jax.nn.sigmoid(scaled)).astype(BF16)


def moved(rows, step):
    cols = rows.shape[0]
    index = lax.broadcasted_iota(jnp.int32, rows.shape, 0)
    edge = 0 if step == 1 else cols - 1
    return jnp.where(index == edge, 0.0, pltpu.roll(rows, step % cols, 0))


def conv_rows(place, halos, rows, sources):
    lead = halos - 1
    sums = []
    for q in range(rows):
        lefts, rights = [], []
        for weight, field in sources:
            for dh in range(3):
                s = lead + q + dh - 1
                if s in field:
                    lefts.append(field[s]())
                    tap = in_order(place, dh, 3)
                    rights.append(jnp.concatenate([weight[tap, dw] for dw in range(3)], axis=-1))
        if not lefts:
            sums.append(None)
            continue
        total = jnp.dot(
            jnp.concatenate(lefts, axis=-1), jnp.concatenate(rights, axis=0), preferred_element_type=F32
        )
        chans = total.shape[1] // 3
        sums.append(
            total[:, chans : 2 * chans]
            + moved(total[:, :chans], 1)
            + moved(total[:, 2 * chans :], -1)
        )
    return sums


def hold(act, slot, value):
    act[slot] = value
    return lambda: act[slot]


def parts_row(halos, rows, near, rest, q):
    if halos == 1:
        return near[0] if q == rows - 1 else rest[q]
    if q in (0, rows - 1):
        return near[0 if q == 0 else 1]
    return rest[q - 1]


def held_rows(halos, rows, row, gain, act):
    return {halos - 1 + q: hold(act, q, activate(row(q), gain)) for q in range(rows)}


def held_edges(halos, rows, edges, gain, act, slot, known=True):
    where = (rows,) if halos == 1 else (0, rows + 1)
    return {
        s: hold(act, slot + h, activate(jnp.where(known, edges[h], jnp.zeros_like(edges[h])), gain))
        for h, s in enumerate(where)
    }


def split_rows(halos, place, field, near, rest):
    rows = field.shape[0]
    if halos == 2:
        near[0] = field[0]
    near[halos - 1] = field[in_order(place, rows - 1, rows)]
    for i in range(rows - halos):
        rest[i] = field[in_order(place, halos - 1 + i, rows)]


def conv_first(halos, place, own, gain, bias, weight, acc, act):
    rows = own.shape[0]
    row = lambda q: own[in_order(place, q, rows)]
    field = held_rows(halos, rows, row, gain[...][None], act)
    for q, part in enumerate(conv_rows(place, halos, rows, [(weight.at[2], field)])):
        acc[q] = part + bias[...][None] + row(q).astype(F32)


def conv_second(halos, place, near2, rest2, odd, edges, odd_edges, before, gain, weight, acc, act):
    rows = before.shape[0]

    @pl.when(place[4] == 0)
    def _():
        sides = [one_back(place, odd_edges[h], odd_edges[h]) for h in range(halos)]
        row = lambda q: one_back(place, odd[q], odd[in_order(place, q, rows)])
        field = held_rows(halos, rows, row, gain[...][None], act)
        field.update(held_edges(halos, rows, sides, gain[...][None], act, rows))
        field2 = held_edges(halos, rows, edges, gain[...][None], act, rows + halos)
        for q, part in enumerate(conv_rows(place, halos, rows, [(weight.at[1], field), (weight.at[2], field2)])):
            acc[q] = before[q] + part

    @pl.when(place[4] != 0)
    def _():
        row = lambda q: parts_row(halos, rows, near2, rest2, q)
        field = held_rows(halos, rows, row, gain[...][None], act)
        for q, part in enumerate(conv_rows(place, halos, rows, [(weight.at[0], field)])):
            acc[q] = before[q] + part


def one_back(place, even, odd):
    none = jnp.zeros_like(odd)
    return jnp.where(place[3] != 0, odd, jnp.where(place[4] != 0, even, none))


def conv_third(halos, place, even_near, even_rest, odd, before, gain, weight, acc, act):
    rows = before.shape[0]

    @pl.when(place[4] == 0)
    def _():
        acc[...] = before[...]

    @pl.when(place[4] != 0)
    def _():
        def row(q):
            return one_back(place, parts_row(halos, rows, even_near, even_rest, q), odd[in_order(place, q, rows)])

        field = held_rows(halos, rows, row, gain[...][None], act)
        for q, part in enumerate(conv_rows(place, halos, rows, [(weight.at[1], field)])):
            acc[q] = before[q] + part


def conv_edges(halos, place, edges, edges2, even_edges, odd_edges, before, gain, weight, block, near, rest, act):
    rows = block.shape[0]

    def give(q, value):
        block[in_order(place, q, rows)] = value
        if q == rows - 1:
            near[halos - 1] = value
        elif q == 0 and halos == 2:
            near[0] = value
        else:
            rest[q - (halos - 1)] = value

    @pl.when(place[4] == 0)
    def _():
        for q in range(rows):
            give(q, before[q].astype(BF16))

    @pl.when(place[4] != 0)
    def _():
        sides = [one_back(place, even_edges[h], odd_edges[h]) for h in range(halos)]
        fields = [
            (weight.at[dt], held_edges(halos, rows, field, gain[...][None], act, dt * halos))
            for dt, field in ((2, edges), (1, sides), (0, edges2))
        ]
        for q, part in enumerate(conv_rows(place, halos, rows, fields)):
            give(q, (before[q] if part is None else before[q] + part).astype(BF16))


def up_rows(place, rows, out_rows, pairs, ubias, uw, wide, outs, out_hbm, osems):
    cols = wide.shape[2] // 2
    rest = ubias.shape[-1] - LANES
    chans = uw.shape[1] // 2
    lane = lax.broadcasted_iota(jnp.int32, (cols, LANES), 1)
    stores = []
    for slot_o, o in enumerate(out_rows):
        phase, taken = pairs[o]
        left = jnp.concatenate([jnp.concatenate([r[f] for r in taken], axis=-1) for f in range(2)], axis=0)
        right = uw[phase, (2 - len(taken)) * chans :, :]
        both = jnp.dot(left, right, preferred_element_type=F32)
        for f in range(2):
            part = both[f * cols : (f + 1) * cols]
            g = [part[:, k * LANES : (k + 1) * LANES] for k in range(6)]
            tail = g[4] + jnp.where(lane < rest, moved(g[5], 1), moved(g[5], -1))
            slot = f
            wide[slot, 0, pl.ds(0, cols, stride=2), :] = g[0] + moved(g[2], 1) + ubias[:LANES][None]
            wide[slot, 0, pl.ds(1, cols, stride=2), :] = g[1] + moved(g[3], -1) + ubias[:LANES][None]
            wide[slot, 1, pl.ds(0, cols, stride=2), :] = tail
            wide[slot, 1, pl.ds(1, cols, stride=2), :] = pltpu.roll(tail, LANES - rest, 1)
            outs[f, slot_o, :LANES, :] = wide[slot, 0].T.astype(BF16)
            outs[f, slot_o, LANES:, :] = (wide[slot, 1, :, :rest] + ubias[LANES:][None]).T.astype(BF16)
            copy = pltpu.make_async_copy(
                outs.at[f, slot_o], out_hbm.at[f, in_order(place, o, 2 * rows)], osems.at[f, slot_o]
            )
            copy.start()
            stores.append(copy)
    return stores


def doubled_rows(lefts, tw, tbias, keep):
    cols = lefts[0].shape[0]
    chans = tw.shape[1] // 2
    mixed = jnp.dot(jnp.concatenate(lefts, axis=0), tw[...], preferred_element_type=F32) + tbias[...][None]
    for i in range(len(lefts)):
        for f in range(2):
            keep(i, f, mixed[i * cols : (i + 1) * cols, f * chans : (f + 1) * chans])


def inside(place, halos, h, value):
    return jnp.where(place[1 + h] == 1, value, 0.0) if halos == 2 else value


def row_pairs(halos, rows, at, out_rows):
    lead = halos - 1
    pairs = {}
    for o in out_rows:
        q, phase = divmod(o, 2)
        sources = [s for s in (lead + q - 1 + phase, lead + q + phase) if s >= 0]
        pairs[o] = phase, [[at(s, f) for f in range(2)] for s in sources]
    return pairs


def inner_rows(halos, rows):
    inner = list(range(0 if halos == 1 else 1, 2 * rows - 1))
    return inner, [o for o in range(2 * rows) if o not in inner]


def first_rows(halos, rows):
    inner, outer = inner_rows(halos, rows)
    half = (len(inner) + 1) // 2
    return inner[:half], inner[half:], outer


def merge_and_first(halos, place, taps, own, odd, tbias, ubias, tw, uw, out_hbm, kept, wide, outs, osems):
    merge_taps(place, taps, uw)

    @pl.when(place[4] == 0)
    def _():
        rows = own.shape[0]
        lead = halos - 1
        lefts = []
        for q in range(rows):
            now, before = own[in_order(place, q, rows)], odd[in_order(place, q, rows)]
            none = jnp.zeros_like(now)
            lefts.append(jnp.concatenate([none, jnp.where(place[3] == 0, none, before), now], axis=-1))

        def keep(q, f, value):
            kept[f, q] = value.astype(BF16)

        doubled_rows(lefts, tw, tbias, keep)
        out_rows = first_rows(halos, rows)[0]
        pairs = row_pairs(halos, rows, lambda s, f: kept[f, s - lead], out_rows)
        for copy in up_rows(place, rows, out_rows, pairs, ubias, uw, wide, outs, out_hbm, osems):
            copy.wait()


def first_middle(halos, place, kept, ubias, uw, out_so_far, out_hbm, token, wide, outs, osems):
    del out_so_far
    token[...] = jnp.zeros_like(token)

    @pl.when(place[4] == 0)
    def _():
        rows = out_hbm.shape[1] // 2
        out_rows = first_rows(halos, rows)[1]
        pairs = row_pairs(halos, rows, lambda s, f: kept[f, s - (halos - 1)], out_rows)
        for copy in up_rows(place, rows, out_rows, pairs, ubias, uw, wide, outs, out_hbm, osems):
            copy.wait()


def first_edges(halos, place, edges, odd_edges, kept, tbias, ubias, tw, uw, token_before, out_so_far,
                out_hbm, token, doubled, wide, outs, osems):
    del token_before, out_so_far
    token[...] = jnp.zeros_like(token)

    @pl.when(place[4] == 0)
    def _():
        rows = out_hbm.shape[1] // 2
        lead = halos - 1
        lefts = []
        for h in range(halos):
            none = jnp.zeros_like(edges[h])
            lefts.append(jnp.concatenate([none, jnp.where(place[3] == 0, none, odd_edges[h]), edges[h]], axis=-1))

        def keep(h, f, value):
            doubled[f, h] = inside(place, halos, h, value).astype(BF16)

        doubled_rows(lefts, tw, tbias, keep)

        def at(s, f):
            if lead <= s < lead + rows:
                return kept[f, s - lead]
            return doubled[f, 0 if s < lead else halos - 1]

        out_rows = first_rows(halos, rows)[2]
        pairs = row_pairs(halos, rows, at, out_rows)
        for copy in up_rows(place, rows, out_rows, pairs, ubias, uw, wide, outs, out_hbm, osems):
            copy.wait()


def up_kernel(halos, place, own, near2, rest2, even_near, even_rest, odd, edges, edges2, even_edges, odd_edges,
              tbias, ubias, tw, uw, token, out_so_far, out_hbm, doubled, wide, outs, osems):
    del token, out_so_far

    @pl.when(place[4] != 0)
    def _():
        rows = own.shape[0]
        lead = halos - 1
        lefts = []
        for s in range(rows + halos):
            if lead <= s < lead + rows:
                q = s - lead
                now, mine = own[in_order(place, q, rows)], odd[in_order(place, q, rows)]
                theirs = parts_row(halos, rows, even_near, even_rest, q)
                first = parts_row(halos, rows, near2, rest2, q)
            else:
                h = 0 if s < lead else halos - 1
                now, mine, theirs, first = edges[h], odd_edges[h], even_edges[h], edges2[h]
            lefts.append(jnp.concatenate([first, jnp.where(place[3] == 0, theirs, mine), now], axis=-1))

        def keep(s, f, value):
            if not lead <= s < lead + rows:
                value = inside(place, halos, 0 if s < lead else halos - 1, value)
            doubled[f, s] = value.astype(BF16)

        doubled_rows(lefts, tw, tbias, keep)
        out_rows = range(2 * rows)
        pairs = row_pairs(halos, rows, lambda s, f: doubled[f, s], out_rows)
        for copy in up_rows(place, rows, out_rows, pairs, ubias, uw, wide, outs, out_hbm, osems):
            copy.wait()


def merge_taps(place, taps, merged):
    chans = taps.shape[3]

    def tap(dh, dw):
        return taps[in_order(place, dh, 3), dw].astype(F32)

    for phase, sets in enumerate((((0,), (1, 2)), ((0, 1), (2,)))):
        for which, rows in enumerate(sets):
            cols = [sum(tap(dh, dw) for dh in rows) for dw in range(3)]
            groups = (cols[1] + cols[2], cols[0] + cols[1], cols[0], cols[2])
            wide = jnp.concatenate([g[:LANES] for g in groups] + [g[LANES:] for g in groups], axis=0)
            merged[phase, which * chans : (which + 1) * chans, :] = wide.T.astype(BF16)


def in_hbm(array):
    return pltpu.with_memory_space_constraint(array, pltpu.HBM)


def together(*arrays):
    return lax.optimization_barrier(arrays)


def in_chip(array):
    return lax.ppermute(array, "tm", [(i, i ^ 1) for i in range(lax.axis_size("tm"))])


def two_back(array):
    frames = lax.axis_size("tm")
    return lax.ppermute(array, "tm", [(i, (i + 2) % frames) for i in range(frames)])


def beside(near):
    tiles = lax.axis_size("tile")
    if tiles == 2:
        return lax.ppermute(near, "tile", [(0, 1), (1, 0)])
    return jnp.concatenate(
        [
            lax.ppermute(near[1:], "tile", [(j, j + 1) for j in range(tiles - 1)]),
            lax.ppermute(near[:1], "tile", [(j + 1, j) for j in range(tiles - 1)]),
        ]
    )


def local(latent, gain, conv_weight, conv_bias, time_weight, time_bias, up_weight, up_bias):
    tiles = lax.axis_size("tile")
    tile = lax.axis_index("tile")
    frame_at = lax.axis_index("tm")
    halos = 1 if tiles == 2 else 2
    main = latent[0]
    rows, cols, chans = main.shape
    outs_n = up_weight.shape[3]
    flip = tile if halos == 1 else 0 * tile
    place = jnp.stack([flip, tile > 0, tile < tiles - 1, frame_at % 2, frame_at >= 2]).astype(jnp.int32)

    def call(kernel, name, share, ins, outs, scratch, **rest):
        return pl.pallas_call(
            kernel,
            out_shape=tuple(s for s, _ in outs),
            in_specs=[SMEM] + ins,
            out_specs=tuple(s for _, s in outs),
            scratch_shapes=scratch,
            compiler_params=pltpu.CompilerParams(vmem_limit_bytes=20 << 20),
            cost_estimate=pl.CostEstimate(
                flops=int(SHARE * share), bytes_accessed=1000, transcendentals=0
            ),
            name=name,
            **rest,
        )

    field = (rows, cols, chans)
    sides = (halos, cols, chans)

    def conv(kernel, name, share, count, more=0):
        step = call(
            functools.partial(kernel, halos), name, share,
            [VMEM] * count,
            [(pltpu.VMEM(field, F32), VMEM)],
            [pltpu.VMEM((rows + more, cols, chans), BF16)],
        )
        return lambda *arrays: step(*arrays)[0]

    taps_t = up_weight.transpose(0, 1, 3, 2)
    near_rest = [
        (jax.ShapeDtypeStruct(sides, BF16), VMEM),
        (jax.ShapeDtypeStruct((max(rows - halos, 1), cols, chans), BF16), VMEM),
    ]
    if rows == halos:
        other = lambda near, rest, move: near
    else:
        other = lambda near, rest, move: move(rest)

    near, rest = call(functools.partial(split_rows, halos), "split_rows", SPLIT, [VMEM], near_rest, [])(place, in_hbm(main))
    near2 = two_back(near)
    edges = beside(near)
    odd = in_chip(main)
    rest2 = other(near2, rest, two_back)
    acc = conv(conv_first, "conv_own_frame", OWN, 4)(place, main, gain, conv_bias, conv_weight)
    near2, edges, acc = together(near2, edges, acc)
    edges2 = beside(near2)
    odd_edges = in_chip(edges)
    even_near = in_chip(near2)
    even_rest = other(even_near, rest2, in_chip)
    acc = conv(conv_second, "conv_two_back", TWO, 8, 2 * halos)(
        place, near2, rest2, odd, edges, odd_edges, acc, gain, conv_weight
    )
    edges2, acc = together(edges2, acc)
    even_edges = in_chip(edges2)
    acc = conv(conv_third, "conv_one_back", THREE, 6)(place, even_near, even_rest, odd, acc, gain, conv_weight)
    block, near, rest = call(
        functools.partial(conv_edges, halos), "conv_edge_rows", 1,
        [VMEM] * 7,
        [(jax.ShapeDtypeStruct(field, BF16), VMEM)] + near_rest,
        [pltpu.VMEM((3 * halos, cols, chans), BF16)],
    )(place, edges, edges2, even_edges, odd_edges, acc, gain, conv_weight)

    near2 = two_back(near)
    edges = beside(near)
    odd = in_chip(block)
    taps_t, main = together(taps_t, block)
    tw = time_weight.reshape(3 * chans, 2 * chans)
    out_shape = (jax.ShapeDtypeStruct((2, 2 * rows, outs_n, 2 * cols), BF16), ANY)

    def scratch(count, held):
        return [
            pltpu.VMEM((2, held, cols, chans), BF16),
            pltpu.VMEM((2, 2, 2 * cols, LANES), F32),
            pltpu.VMEM((2, count, outs_n, 2 * cols), BF16),
            pltpu.SemaphoreType.DMA((2, count)),
        ]

    rest2 = other(near2, rest, two_back)
    one, two, three = (len(o) for o in first_rows(halos, rows))
    merged, out, kept = call(
        functools.partial(merge_and_first, halos), "merge_taps_and_first_chip_rows", MERGE,
        [VMEM] * 6,
        [
            (pltpu.VMEM((2, 2 * chans, 4 * outs_n), BF16), VMEM),
            out_shape,
            (pltpu.VMEM((2,) + field, BF16), VMEM),
        ],
        scratch(one, rows)[1:],
    )(place, taps_t, main, odd, time_bias, up_bias, tw)
    common = (time_bias, up_bias, tw, merged)
    near2, kept = together(near2, kept)
    edges2 = beside(near2)
    edges, near2 = together(edges, near2)
    odd_edges = in_chip(edges)
    near2, rest2, kept = together(near2, rest2, kept)
    even_near = in_chip(near2)
    even_rest = other(even_near, rest2, in_chip)
    token_spec = (jax.ShapeDtypeStruct((8, LANES), F32), VMEM)
    out, token = call(
        functools.partial(first_middle, halos), "first_chip_middle_rows", FIRST,
        [VMEM] * 3 + [ANY],
        [out_shape, token_spec],
        scratch(two, halos)[1:],
        input_output_aliases={4: 0},
    )(place, kept, up_bias, merged, out)
    edges2, token = together(edges2, token)
    out, token = call(
        functools.partial(first_edges, halos), "first_chip_edge_rows", FIRST,
        [VMEM] * 7 + [ANY] * 2,
        [out_shape, token_spec],
        scratch(three, halos),
        input_output_aliases={9: 0},
    )(place, edges, odd_edges, kept, *common, token, out)
    even_edges = in_chip(edges2)
    (out,) = call(
        functools.partial(up_kernel, halos), "time_and_up", 1,
        [VMEM] * 14 + [ANY] * 2,
        [out_shape],
        scratch(2 * rows, rows + halos),
        input_output_aliases={16: 0},
    )(place, main, near2, rest2, even_near, even_rest, odd, edges, edges2, even_edges, odd_edges,
      *common, token, out)
    return out.transpose(0, 1, 3, 2)


def solution(mesh):
    placed = (P("tm", "tile", None, None), P(), P(), P(), P(), P(), P(), P())
    return jax.shard_map(
        local, mesh=mesh, in_specs=placed, out_specs=P("tm", "tile", None, None), check_vma=False
    )
```

```python
import functools

import jax
import jax.numpy as jnp
from jax import lax
from jax.experimental import pallas as pl
from jax.experimental.pallas import tpu as pltpu
from jax.sharding import PartitionSpec as P

F32 = jnp.float32
BF16 = jnp.bfloat16
VMEM = pl.BlockSpec(memory_space=pltpu.VMEM)
SMEM = pl.BlockSpec(memory_space=pltpu.SMEM)
ANY = pl.BlockSpec(memory_space=pl.ANY)
HBM = pl.BlockSpec(memory_space=pltpu.HBM)
LANES = 128
SHARE = 3000000000
SPLIT = 1
OWN = 0.2
TWO = 0.2
THREE = 1
MERGE = 0.2
FIRST = 0.01


def in_order(place, index, count):
    return jnp.where(place[0] == 1, count - 1 - index, index)


def activate(rows, gain):
    values = rows.astype(F32)
    meansq = jnp.mean(values * values, axis=-1, keepdims=True)
    scaled = values * lax.rsqrt(meansq + 1e-06) * gain
    return (scaled * jax.nn.sigmoid(scaled)).astype(BF16)


def moved(rows, step):
    cols = rows.shape[0]
    index = lax.broadcasted_iota(jnp.int32, rows.shape, 0)
    edge = 0 if step == 1 else cols - 1
    return jnp.where(index == edge, 0.0, pltpu.roll(rows, step % cols, 0))


def conv_rows(place, halos, rows, sources):
    lead = halos - 1
    sums = []
    for q in range(rows):
        lefts, rights = [], []
        for weight, field in sources:
            for dh in range(3):
                s = lead + q + dh - 1
                if s in field:
                    lefts.append(field[s]())
                    tap = in_order(place, dh, 3)
                    rights.append(jnp.concatenate([weight[tap, dw] for dw in range(3)], axis=-1))
        if not lefts:
            sums.append(None)
            continue
        total = jnp.dot(
            jnp.concatenate(lefts, axis=-1), jnp.concatenate(rights, axis=0), preferred_element_type=F32
        )
        chans = total.shape[1] // 3
        sums.append(
            total[:, chans : 2 * chans]
            + moved(total[:, :chans], 1)
            + moved(total[:, 2 * chans :], -1)
        )
    return sums


def hold(act, slot, value):
    act[slot] = value
    return lambda: act[slot]


def parts_row(halos, rows, near, rest, q):
    if halos == 1:
        return near[0] if q == rows - 1 else rest[q]
    if q in (0, rows - 1):
        return near[0 if q == 0 else 1]
    return rest[q - 1]


def held_rows(halos, rows, row, gain, act):
    return {halos - 1 + q: hold(act, q, activate(row(q), gain)) for q in range(rows)}


def held_edges(halos, rows, edges, gain, act, slot, known=True):
    where = (rows,) if halos == 1 else (0, rows + 1)
    return {
        s: hold(act, slot + h, activate(jnp.where(known, edges[h], jnp.zeros_like(edges[h])), gain))
        for h, s in enumerate(where)
    }


def split_rows(halos, place, field, near, rest):
    rows = field.shape[0]
    if halos == 2:
        near[0] = field[0]
    near[halos - 1] = field[in_order(place, rows - 1, rows)]
    for i in range(rows - halos):
        rest[i] = field[in_order(place, halos - 1 + i, rows)]


def conv_first(halos, place, own, gain, bias, weight, acc, act):
    rows = own.shape[0]
    row = lambda q: own[in_order(place, q, rows)]
    field = held_rows(halos, rows, row, gain[...][None], act)
    for q, part in enumerate(conv_rows(place, halos, rows, [(weight.at[2], field)])):
        acc[q] = part + bias[...][None] + row(q).astype(F32)


def conv_second(halos, place, near2, rest2, odd, edges, odd_edges, before, gain, weight, acc, act):
    rows = before.shape[0]

    @pl.when(place[4] == 0)
    def _():
        sides = [one_back(place, odd_edges[h], odd_edges[h]) for h in range(halos)]
        row = lambda q: one_back(place, odd[q], odd[in_order(place, q, rows)])
        field = held_rows(halos, rows, row, gain[...][None], act)
        field.update(held_edges(halos, rows, sides, gain[...][None], act, rows))
        field2 = held_edges(halos, rows, edges, gain[...][None], act, rows + halos)
        for q, part in enumerate(conv_rows(place, halos, rows, [(weight.at[1], field), (weight.at[2], field2)])):
            acc[q] = before[q] + part

    @pl.when(place[4] != 0)
    def _():
        row = lambda q: parts_row(halos, rows, near2, rest2, q)
        field = held_rows(halos, rows, row, gain[...][None], act)
        for q, part in enumerate(conv_rows(place, halos, rows, [(weight.at[0], field)])):
            acc[q] = before[q] + part


def one_back(place, even, odd):
    none = jnp.zeros_like(odd)
    return jnp.where(place[3] != 0, odd, jnp.where(place[4] != 0, even, none))


def conv_third(halos, place, even_near, even_rest, odd, before, gain, weight, acc, act):
    rows = before.shape[0]

    @pl.when(place[4] == 0)
    def _():
        acc[...] = before[...]

    @pl.when(place[4] != 0)
    def _():
        def row(q):
            return one_back(place, parts_row(halos, rows, even_near, even_rest, q), odd[in_order(place, q, rows)])

        field = held_rows(halos, rows, row, gain[...][None], act)
        for q, part in enumerate(conv_rows(place, halos, rows, [(weight.at[1], field)])):
            acc[q] = before[q] + part


def conv_edges(halos, place, edges, edges2, even_edges, odd_edges, before, gain, weight, block, near, rest, act):
    rows = block.shape[0]

    def give(q, value):
        block[in_order(place, q, rows)] = value
        if q == rows - 1:
            near[halos - 1] = value
        elif q == 0 and halos == 2:
            near[0] = value
        else:
            rest[q - (halos - 1)] = value

    @pl.when(place[4] == 0)
    def _():
        for q in range(rows):
            give(q, before[q].astype(BF16))

    @pl.when(place[4] != 0)
    def _():
        sides = [one_back(place, even_edges[h], odd_edges[h]) for h in range(halos)]
        fields = [
            (weight.at[dt], held_edges(halos, rows, field, gain[...][None], act, dt * halos))
            for dt, field in ((2, edges), (1, sides), (0, edges2))
        ]
        for q, part in enumerate(conv_rows(place, halos, rows, fields)):
            give(q, (before[q] if part is None else before[q] + part).astype(BF16))


def up_rows(place, rows, out_rows, pairs, ubias, uw, wide, outs, out_hbm, osems):
    cols = wide.shape[2] // 2
    rest = ubias.shape[-1] - LANES
    chans = uw.shape[1] // 2
    lane = lax.broadcasted_iota(jnp.int32, (cols, LANES), 1)
    stores = []
    for slot_o, o in enumerate(out_rows):
        phase, taken = pairs[o]
        left = jnp.concatenate([jnp.concatenate([r[f] for r in taken], axis=-1) for f in range(2)], axis=0)
        right = uw[phase, (2 - len(taken)) * chans :, :]
        both = jnp.dot(left, right, preferred_element_type=F32)
        for f in range(2):
            part = both[f * cols : (f + 1) * cols]
            g = [part[:, k * LANES : (k + 1) * LANES] for k in range(6)]
            tail = g[4] + jnp.where(lane < rest, moved(g[5], 1), moved(g[5], -1))
            slot = f
            wide[slot, 0, pl.ds(0, cols, stride=2), :] = g[0] + moved(g[2], 1) + ubias[:LANES][None]
            wide[slot, 0, pl.ds(1, cols, stride=2), :] = g[1] + moved(g[3], -1) + ubias[:LANES][None]
            wide[slot, 1, pl.ds(0, cols, stride=2), :] = tail
            wide[slot, 1, pl.ds(1, cols, stride=2), :] = pltpu.roll(tail, LANES - rest, 1)
            outs[f, slot_o, :LANES, :] = wide[slot, 0].T.astype(BF16)
            outs[f, slot_o, LANES:, :] = (wide[slot, 1, :, :rest] + ubias[LANES:][None]).T.astype(BF16)
            copy = pltpu.make_async_copy(
                outs.at[f, slot_o], out_hbm.at[f, in_order(place, o, 2 * rows)], osems.at[f, slot_o]
            )
            copy.start()
            stores.append(copy)
    return stores


def doubled_rows(lefts, tw, tbias, keep):
    cols = lefts[0].shape[0]
    chans = tw.shape[1] // 2
    mixed = jnp.dot(jnp.concatenate(lefts, axis=0), tw[...], preferred_element_type=F32) + tbias[...][None]
    for i in range(len(lefts)):
        for f in range(2):
            keep(i, f, mixed[i * cols : (i + 1) * cols, f * chans : (f + 1) * chans])


def inside(place, halos, h, value):
    return jnp.where(place[1 + h] == 1, value, 0.0) if halos == 2 else value


def row_pairs(halos, rows, at, out_rows):
    lead = halos - 1
    pairs = {}
    for o in out_rows:
        q, phase = divmod(o, 2)
        sources = [s for s in (lead + q - 1 + phase, lead + q + phase) if s >= 0]
        pairs[o] = phase, [[at(s, f) for f in range(2)] for s in sources]
    return pairs


def inner_rows(halos, rows):
    inner = list(range(0 if halos == 1 else 1, 2 * rows - 1))
    return inner, [o for o in range(2 * rows) if o not in inner]


def first_rows(halos, rows):
    inner, outer = inner_rows(halos, rows)
    half = (len(inner) + 1) // 2
    return inner[:half], inner[half:] + outer


def merge_and_first(halos, place, taps, own, odd, tbias, ubias, tw, uw, out_hbm, kept, wide, outs, osems):
    merge_taps(place, taps, uw)

    @pl.when(place[4] == 0)
    def _():
        rows = own.shape[0]
        lead = halos - 1
        lefts = []
        for q in range(rows):
            now, before = own[in_order(place, q, rows)], odd[in_order(place, q, rows)]
            none = jnp.zeros_like(now)
            lefts.append(jnp.concatenate([none, jnp.where(place[3] == 0, none, before), now], axis=-1))

        def keep(q, f, value):
            kept[f, q] = value.astype(BF16)

        doubled_rows(lefts, tw, tbias, keep)
        out_rows = first_rows(halos, rows)[0]
        pairs = row_pairs(halos, rows, lambda s, f: kept[f, s - lead], out_rows)
        for copy in up_rows(place, rows, out_rows, pairs, ubias, uw, wide, outs, out_hbm, osems):
            copy.wait()


def first_edges(halos, place, edges, odd_edges, kept, tbias, ubias, tw, uw, out_so_far,
                out_hbm, token, doubled, wide, outs, osems):
    del out_so_far
    token[...] = jnp.zeros_like(token)

    @pl.when(place[4] == 0)
    def _():
        rows = out_hbm.shape[1] // 2
        lead = halos - 1
        lefts = []
        for h in range(halos):
            none = jnp.zeros_like(edges[h])
            lefts.append(jnp.concatenate([none, jnp.where(place[3] == 0, none, odd_edges[h]), edges[h]], axis=-1))

        def keep(h, f, value):
            doubled[f, h] = inside(place, halos, h, value).astype(BF16)

        doubled_rows(lefts, tw, tbias, keep)

        def at(s, f):
            if lead <= s < lead + rows:
                return kept[f, s - lead]
            return doubled[f, 0 if s < lead else halos - 1]

        out_rows = first_rows(halos, rows)[1]
        pairs = row_pairs(halos, rows, at, out_rows)
        for copy in up_rows(place, rows, out_rows, pairs, ubias, uw, wide, outs, out_hbm, osems):
            copy.wait()


def up_kernel(halos, place, own, near2, rest2, even_near, even_rest, odd, edges, edges2, even_edges, odd_edges,
              tbias, ubias, tw, uw, token, out_so_far, out_hbm, doubled, wide, outs, osems):
    del token, out_so_far

    @pl.when(place[4] != 0)
    def _():
        rows = own.shape[0]
        lead = halos - 1
        lefts = []
        for s in range(rows + halos):
            if lead <= s < lead + rows:
                q = s - lead
                now, mine = own[in_order(place, q, rows)], odd[in_order(place, q, rows)]
                theirs = parts_row(halos, rows, even_near, even_rest, q)
                first = parts_row(halos, rows, near2, rest2, q)
            else:
                h = 0 if s < lead else halos - 1
                now, mine, theirs, first = edges[h], odd_edges[h], even_edges[h], edges2[h]
            lefts.append(jnp.concatenate([first, jnp.where(place[3] == 0, theirs, mine), now], axis=-1))

        def keep(s, f, value):
            if not lead <= s < lead + rows:
                value = inside(place, halos, 0 if s < lead else halos - 1, value)
            doubled[f, s] = value.astype(BF16)

        doubled_rows(lefts, tw, tbias, keep)
        out_rows = range(2 * rows)
        pairs = row_pairs(halos, rows, lambda s, f: doubled[f, s], out_rows)
        for copy in up_rows(place, rows, out_rows, pairs, ubias, uw, wide, outs, out_hbm, osems):
            copy.wait()


def merge_taps(place, taps, merged):
    chans = taps.shape[3]

    def tap(dh, dw):
        return taps[in_order(place, dh, 3), dw].astype(F32)

    for phase, sets in enumerate((((0,), (1, 2)), ((0, 1), (2,)))):
        for which, rows in enumerate(sets):
            cols = [sum(tap(dh, dw) for dh in rows) for dw in range(3)]
            groups = (cols[1] + cols[2], cols[0] + cols[1], cols[0], cols[2])
            wide = jnp.concatenate([g[:LANES] for g in groups] + [g[LANES:] for g in groups], axis=0)
            merged[phase, which * chans : (which + 1) * chans, :] = wide.T.astype(BF16)


def in_hbm(array):
    return pltpu.with_memory_space_constraint(array, pltpu.HBM)


def together(*arrays):
    return lax.optimization_barrier(arrays)


def in_chip(array):
    return lax.ppermute(array, "tm", [(i, i ^ 1) for i in range(lax.axis_size("tm"))])


def two_back(array):
    frames = lax.axis_size("tm")
    return lax.ppermute(array, "tm", [(i, (i + 2) % frames) for i in range(frames)])


def beside(near):
    tiles = lax.axis_size("tile")
    if tiles == 2:
        return lax.ppermute(near, "tile", [(0, 1), (1, 0)])
    return jnp.concatenate(
        [
            lax.ppermute(near[1:], "tile", [(j, j + 1) for j in range(tiles - 1)]),
            lax.ppermute(near[:1], "tile", [(j + 1, j) for j in range(tiles - 1)]),
        ]
    )


def local(latent, gain, conv_weight, conv_bias, time_weight, time_bias, up_weight, up_bias):
    tiles = lax.axis_size("tile")
    tile = lax.axis_index("tile")
    frame_at = lax.axis_index("tm")
    halos = 1 if tiles == 2 else 2
    main = latent[0]
    rows, cols, chans = main.shape
    outs_n = up_weight.shape[3]
    flip = tile if halos == 1 else 0 * tile
    place = jnp.stack([flip, tile > 0, tile < tiles - 1, frame_at % 2, frame_at >= 2]).astype(jnp.int32)

    def call(kernel, name, share, ins, outs, scratch, **rest):
        return pl.pallas_call(
            kernel,
            out_shape=tuple(s for s, _ in outs),
            in_specs=[SMEM] + ins,
            out_specs=tuple(s for _, s in outs),
            scratch_shapes=scratch,
            compiler_params=pltpu.CompilerParams(vmem_limit_bytes=32 << 20),
            cost_estimate=pl.CostEstimate(
                flops=int(SHARE * share), bytes_accessed=1000, transcendentals=0
            ),
            name=name,
            **rest,
        )

    field = (rows, cols, chans)
    sides = (halos, cols, chans)

    def conv(kernel, name, share, count, more=0):
        step = call(
            functools.partial(kernel, halos), name, share,
            [VMEM] * count,
            [(pltpu.VMEM(field, F32), VMEM)],
            [pltpu.VMEM((rows + more, cols, chans), BF16)],
        )
        return lambda *arrays: step(*arrays)[0]

    taps_t = up_weight.transpose(0, 1, 3, 2)
    near_rest = [
        (jax.ShapeDtypeStruct(sides, BF16), VMEM),
        (jax.ShapeDtypeStruct((max(rows - halos, 1), cols, chans), BF16), VMEM),
    ]
    if rows == halos:
        other = lambda near, rest, move: near
    else:
        other = lambda near, rest, move: move(rest)

    near, rest = call(functools.partial(split_rows, halos), "split_rows", SPLIT, [VMEM], near_rest, [])(place, in_hbm(main))
    near2 = two_back(near)
    edges = beside(near)
    odd = in_chip(main)
    rest2 = other(near2, rest, two_back)
    acc = conv(conv_first, "conv_own_frame", OWN, 4)(place, main, gain, conv_bias, conv_weight)
    near2, edges, acc = together(near2, edges, acc)
    edges2 = beside(near2)
    odd_edges = in_chip(edges)
    even_near = in_chip(near2)
    even_rest = other(even_near, rest2, in_chip)
    acc = conv(conv_second, "conv_two_back", TWO, 8, 2 * halos)(
        place, near2, rest2, odd, edges, odd_edges, acc, gain, conv_weight
    )
    edges2, acc = together(edges2, acc)
    even_edges = in_chip(edges2)
    acc = conv(conv_third, "conv_one_back", THREE, 6)(place, even_near, even_rest, odd, acc, gain, conv_weight)
    block, near, rest = call(
        functools.partial(conv_edges, halos), "conv_edge_rows", 1,
        [VMEM] * 7,
        [(jax.ShapeDtypeStruct(field, BF16), VMEM)] + near_rest,
        [pltpu.VMEM((3 * halos, cols, chans), BF16)],
    )(place, edges, edges2, even_edges, odd_edges, acc, gain, conv_weight)

    near2 = two_back(near)
    edges = beside(near)
    odd = in_chip(block)
    taps_t, main = together(taps_t, block)
    tw = time_weight.reshape(3 * chans, 2 * chans)
    out_shape = (jax.ShapeDtypeStruct((2, 2 * rows, outs_n, 2 * cols), BF16), ANY)

    def scratch(count, held):
        return [
            pltpu.VMEM((2, held, cols, chans), BF16),
            pltpu.VMEM((2, 2, 2 * cols, LANES), F32),
            pltpu.VMEM((2, count, outs_n, 2 * cols), BF16),
            pltpu.SemaphoreType.DMA((2, count)),
        ]

    rest2 = other(near2, rest, two_back)
    one, two = (len(o) for o in first_rows(halos, rows))
    merged, out, kept = call(
        functools.partial(merge_and_first, halos), "merge_taps_and_first_chip_rows", MERGE,
        [VMEM] * 6,
        [
            (pltpu.VMEM((2, 2 * chans, 4 * outs_n), BF16), VMEM),
            out_shape,
            (pltpu.VMEM((2,) + field, BF16), VMEM),
        ],
        scratch(one, rows)[1:],
    )(place, taps_t, main, odd, time_bias, up_bias, tw)
    common = (time_bias, up_bias, tw, merged)
    near2, kept = together(near2, kept)
    edges2 = beside(near2)
    edges, near2 = together(edges, near2)
    odd_edges = in_chip(edges)
    near2, rest2, kept = together(near2, rest2, kept)
    even_near = in_chip(near2)
    even_rest = other(even_near, rest2, in_chip)
    out, token = call(
        functools.partial(first_edges, halos), "first_chip_edge_rows", FIRST,
        [VMEM] * 7 + [ANY],
        [out_shape, (jax.ShapeDtypeStruct((8, LANES), F32), VMEM)],
        scratch(two, halos),
        input_output_aliases={8: 0},
    )(place, edges, odd_edges, kept, *common, out)
    even_edges = in_chip(edges2)
    (out,) = call(
        functools.partial(up_kernel, halos), "time_and_up", 1,
        [VMEM] * 14 + [ANY] * 2,
        [out_shape],
        scratch(2 * rows, rows + halos),
        input_output_aliases={16: 0},
    )(place, main, near2, rest2, even_near, even_rest, odd, edges, edges2, even_edges, odd_edges,
      *common, token, out)
    return out.transpose(0, 1, 3, 2)


def solution(mesh):
    placed = (P("tm", "tile", None, None), P(), P(), P(), P(), P(), P(), P())
    return jax.shard_map(
        local, mesh=mesh, in_specs=placed, out_specs=P("tm", "tile", None, None), check_vma=False
    )
```
